32 devices in a mesh: ctx: 8 (over z, x), ch: 4 (over y, core).
Axes of the slice: x: 2, y: 2, z: 4, core: 2. Of those that a mesh axis runs over, the one named last changes fastest.
Arguments:
- query: bfloat16 [1024, 8192], P('ctx', 'ch'), may hold values from -6 to 6
- key: bfloat16 [1024, 8192], P('ctx', 'ch'), may hold values from -6 to 6
- value: bfloat16 [1024, 8192], P('ctx', 'ch'), may hold values from -6 to 6
- filter_taps: bfloat16 [1024, 512], P('ctx', 'ch'), may hold values from -0.1875 to 0.1875
- skip: float32 [8192], P('ch'), may hold values from -1 to 1
Outputs:
- gated: bfloat16 [1024, 8192], P('ctx', 'ch')
The draws below stay inside these ranges and needn't reach their ends.
All inputs are finite; a program needn't handle non-finite values.
Results may differ from the reference program's by a relative error of at most 0.0085.
Values may be sent and summed in bfloat16 or wider, within the bound.
No kernel may reach another device: no remote copies, remote signals or barrier semaphores. Data moves between devices by JAX's collectives and lax.ppermute only.
A program may use at most 192 MiB of HBM per device.

```python
import jax
import jax.numpy as jnp

D = 8192
GROUP = 16
BLOCK = 128
LAGS = 8
TAPS = 1024
GROUPS = 512
LENGTH = 1024


def level_of(key, shape, cuts, smallest, largest):
    def one(position, shards_of):
        steps = jax.random.uniform(jax.random.fold_in(jax.random.fold_in(key, 6), position), (shards_of,), jnp.float32, smallest / len(cuts), largest / len(cuts))
        return jnp.repeat(jnp.exp(steps), shape[position] // shards_of).reshape((-1,) + (1,) * (len(shape) - position - 1))

    loudness = one(*cuts[0])
    for cut in cuts[1:]:
        loudness = loudness * one(*cut)
    return loudness


def scatter_about(key, extent, spread, reach, split=(), held_as=jnp.bfloat16):
    entries = spread * jax.random.normal(key, extent, jnp.float32)
    if split:
        entries = entries * level_of(key, extent, split, -0.22, 0.18)
    return jnp.clip(entries, -reach, reach).astype(held_as)


def setup_inputs(seed: int = 0) -> dict:
    keys = jax.random.split(jax.random.key(seed), 6)
    return {
        "query": scatter_about(keys[0], (LENGTH, D), 1.0, 6.0, ((0, 8), (1, 4))),
        "key": scatter_about(keys[1], (LENGTH, D), 1.0, 6.0, ((0, 8), (1, 4))),
        "value": scatter_about(keys[2], (LENGTH, D), 1.0, 6.0, ((0, 8), (1, 4))),
        "filter_taps": scatter_about(keys[3], (TAPS, GROUPS), TAPS ** -0.5, 0.1875, ((0, 8), (1, 4))),
        "skip": jnp.clip(jax.random.uniform(keys[4], (D,), jnp.float32, -1.0, 1.0) * level_of(keys[4], (D,), ((0, 4),), -0.4, 0.0), -1.0, 1.0),
    }


def reference(query, key, value, filter_taps, skip):
    length = query.shape[0]
    channels = query.shape[1]
    groups = channels // GROUP
    nblocks = length // BLOCK
    mixed = (key.astype(jnp.float32) * value.astype(jnp.float32)).astype(jnp.bfloat16)
    blocks = mixed.astype(jnp.float32).reshape(nblocks, BLOCK, groups, GROUP)
    taps_float = filter_taps.astype(jnp.float32).T
    padded = jnp.concatenate([jnp.zeros((groups, BLOCK), jnp.float32), taps_float, jnp.zeros((groups, BLOCK), jnp.float32)], axis=1)
    offsets = (BLOCK - 1) + jnp.arange(BLOCK)[:, None] - jnp.arange(BLOCK)[None, :]
    summed = jnp.zeros((nblocks, BLOCK, groups, GROUP), jnp.float32)
    for lag_index in range(LAGS):
        window = padded[:, lag_index * BLOCK + 1: lag_index * BLOCK + 1 + 2 * BLOCK]
        toeplitz = window[:, offsets]
        earlier = jnp.concatenate([jnp.zeros((lag_index, BLOCK, groups, GROUP), jnp.float32), blocks[:nblocks - lag_index]], axis=0)
        summed = summed + jnp.einsum('gts,nsgc->ntgc', toeplitz, earlier)
    conv = summed.reshape(length, channels)
    gated = query.astype(jnp.float32) * (conv + skip[None, :] * mixed.astype(jnp.float32))
    return gated.astype(jnp.bfloat16)
```

```python
import jax
import jax.numpy as jnp
from jax import lax
from jax.experimental import pallas as pl
from jax.experimental.pallas import tpu as pltpu
from jax.sharding import PartitionSpec as P

GROUP = 16
BLOCK = 128
LAGS = 8
LANES = 128
TILE = 16
SIDE = LANES // GROUP


def swap_granules(tiles):
    granule = lax.broadcasted_iota(jnp.int32, tiles[0].shape, 1) // GROUP
    tiles = list(tiles)
    for bit in (1, 2, 4):
        high = (granule & bit) != 0
        swapped = list(tiles)
        for low_index in range(SIDE):
            if low_index & bit:
                continue
            low, top = tiles[low_index], tiles[low_index | bit]
            swapped[low_index] = jnp.where(high, pltpu.roll(top, bit * GROUP, 1), low)
            swapped[low_index | bit] = jnp.where(high, top, pltpu.roll(low, LANES - bit * GROUP, 1))
        tiles = swapped
    return tiles


def mix_kernel(parts, key_ref, value_ref, taps_ref, sent_ref):
    width = sent_ref.shape[2]
    tap = lax.broadcasted_iota(jnp.int32, (BLOCK, LANES), 0)
    place = lax.broadcasted_iota(jnp.int32, (BLOCK, LANES), 1)
    mirror = jnp.where((tap + place) % BLOCK == 0, 1.0, 0.0).astype(jnp.bfloat16)
    mirrored = lax.dot_general(
        taps_ref[...], mirror, (((0,), (0,)), ((), ())), preferred_element_type=jnp.float32
    ).astype(jnp.bfloat16)
    for part in range(parts):
        columns = slice(part * width, (part + 1) * width)
        sent_ref[part, 0:BLOCK, :] = (
            key_ref[:, columns].astype(jnp.float32) * value_ref[:, columns].astype(jnp.float32)
        ).astype(jnp.bfloat16)
        own = mirrored[part * TILE : (part + 1) * TILE]
        for start in range(0, width, LANES):
            sent_ref[part, BLOCK : BLOCK + TILE, start : start + LANES] = own


def conv_kernel(sources, *refs):
    got_refs, (conv_ref, *all_gathered, results) = refs[:sources], refs[sources:]
    got_ref, gathered = got_refs[0], all_gathered[0]
    halves = conv_ref.shape[2] // LANES
    for half in range(halves):
        columns = slice(half * LANES, (half + 1) * LANES)

        @pl.loop(0, BLOCK // TILE)
        def _(step):
            rows = pl.ds(pl.multiple_of(step * TILE, TILE), TILE)
            for from_ref, to_ref in zip(got_refs, all_gathered):
                tiles = swap_granules([from_ref[block, rows, columns] for block in range(LAGS)])
                for index in range(SIDE):
                    to_ref[half * SIDE + index, rows, :] = tiles[index]

    lane = lax.broadcasted_iota(jnp.int32, (BLOCK, LANES), 1)
    row = lax.broadcasted_iota(jnp.int32, (BLOCK, LANES), 0)
    causal = row >= lane

    @pl.loop(0, halves * SIDE)
    def _(group):
        source = gathered[group]
        earlier = all_gathered[1][group] if sources > 1 else None
        before = jnp.zeros((BLOCK, LANES), jnp.float32)
        total = None
        filters, shifted = [], []
        for lag in range(LAGS):
            taps = got_ref[lag, BLOCK : BLOCK + TILE, 0:LANES].astype(jnp.float32)
            pick = lax.broadcasted_iota(jnp.int32, (TILE, LANES), 0) == group
            own = jnp.sum(jnp.where(pick, taps, 0.0), axis=0, keepdims=True)
            turned = pltpu.roll(jnp.broadcast_to(own, (BLOCK, LANES)), 0, 1, stride=1, stride_axis=0)
            filters.append(jnp.where(causal, turned, before).astype(jnp.bfloat16))
            before = turned
            if lag:
                moved = pltpu.roll(source, lag * GROUP, 1)
                carried = pltpu.roll(earlier, lag * GROUP, 1) if sources > 1 else jnp.zeros_like(moved)
                shifted.append(jnp.where(lane >= lag * GROUP, moved, carried))
            else:
                shifted.append(source)
        total = jnp.dot(
            jnp.concatenate(filters, axis=1),
            jnp.concatenate(shifted, axis=0),
            preferred_element_type=jnp.float32,
        )
        results[group] = total.astype(jnp.bfloat16)

    for half in range(halves):
        columns = slice(half * LANES, (half + 1) * LANES)

        @pl.loop(0, BLOCK // TILE)
        def _(step):
            rows = pl.ds(pl.multiple_of(step * TILE, TILE), TILE)
            tiles = swap_granules([results[half * SIDE + index, rows, :] for index in range(SIDE)])
            for block in range(LAGS):
                conv_ref[block, rows, columns] = tiles[block]


def gate_kernel(parts, query_ref, sent_ref, conv_ref, skip_ref, gated_ref):
    width = sent_ref.shape[2]
    for part in range(parts):
        columns = slice(part * width, (part + 1) * width)
        mixed = sent_ref[part, 0:BLOCK, :].astype(jnp.float32)
        summed = conv_ref[part].astype(jnp.float32) + skip_ref[:, columns] * mixed
        gated_ref[:, columns] = (query_ref[:, columns].astype(jnp.float32) * summed).astype(jnp.bfloat16)


def per_device(query, key, value, filter_taps, skip):
    rows, channels = query.shape
    parts = LAGS
    width = channels // parts
    count = lax.axis_size("ctx")
    windows = None
    if count > LAGS:
        windows = [list(range(first, first + LAGS)) for first in range(0, count, LAGS)]
        all_taps = lax.all_gather(filter_taps, "ctx", axis=0, tiled=True)
        first_tap = lax.axis_index("ctx") % LAGS * BLOCK
        filter_taps = lax.dynamic_slice_in_dim(all_taps, first_tap, BLOCK, axis=0)
    sent = pl.pallas_call(
        lambda *refs: mix_kernel(parts, *refs),
        out_shape=jax.ShapeDtypeStruct((parts, BLOCK + TILE, width), jnp.bfloat16),
    )(key, value, filter_taps)
    got = [lax.all_to_all(sent, "ctx", 0, 0, tiled=True, axis_index_groups=windows)]
    if count > LAGS:
        onward = [(source, source + LAGS) for source in range(count - LAGS)]
        got.append(lax.ppermute(got[0], "ctx", onward))
    conv = pl.pallas_call(
        lambda *refs: conv_kernel(len(got), *refs),
        out_shape=jax.ShapeDtypeStruct((parts, BLOCK, width), jnp.bfloat16),
        scratch_shapes=[pltpu.VMEM((width // GROUP, BLOCK, LANES), jnp.bfloat16)] * (len(got) + 1),
    )(*got)
    back = lax.all_to_all(conv, "ctx", 0, 0, tiled=True, axis_index_groups=windows)
    return pl.pallas_call(
        lambda *refs: gate_kernel(parts, *refs),
        out_shape=jax.ShapeDtypeStruct((rows, channels), jnp.bfloat16),
    )(query, sent, back, skip.reshape(1, channels))


def solution(mesh):
    placed = (P("ctx", "ch"), P("ctx", "ch"), P("ctx", "ch"), P("ctx", "ch"), P("ch"))
    return jax.shard_map(
        per_device, mesh=mesh, in_specs=placed, out_specs=P("ctx", "ch"), check_vma=False
    )
```

```python
import jax
import jax.numpy as jnp
from jax import lax
from jax.experimental import pallas as pl
from jax.experimental.pallas import tpu as pltpu
from jax.sharding import PartitionSpec as P

GROUP = 16
BLOCK = 128
LAGS = 8
LANES = 128
TILE = 16
SIDE = LANES // GROUP
CHUNKS = 4
SMALL = pltpu.CompilerParams(vmem_limit_bytes=16 * 1024 * 1024)


def mix_kernel(parts, chunks, key_hbm, value_hbm, taps_hbm, sent_hbm, key_ref, value_ref, taps_ref, sent_ref, arrived, left):
    width = sent_ref.shape[2]
    step = parts // chunks
    taps_copy = pltpu.make_async_copy(taps_hbm, taps_ref, arrived.at[2 * chunks])
    taps_copy.start()
    copies = []
    for chunk in range(chunks):
        columns = slice(chunk * step * width, (chunk + 1) * step * width)
        pair = [
            pltpu.make_async_copy(key_hbm.at[:, columns], key_ref.at[:, columns], arrived.at[2 * chunk]),
            pltpu.make_async_copy(value_hbm.at[:, columns], value_ref.at[:, columns], arrived.at[2 * chunk + 1]),
        ]
        for copy in pair:
            copy.start()
        copies.append(pair)
    tap = lax.broadcasted_iota(jnp.int32, (BLOCK, LANES), 0)
    place = lax.broadcasted_iota(jnp.int32, (BLOCK, LANES), 1)
    mirror = jnp.where((tap + place) % BLOCK == 0, 1.0, 0.0).astype(jnp.bfloat16)
    taps_copy.wait()
    mirrored = lax.dot_general(
        taps_ref[...], mirror, (((0,), (0,)), ((), ())), preferred_element_type=jnp.float32
    ).astype(jnp.bfloat16)
    for part in range(parts):
        own = mirrored[part * TILE : (part + 1) * TILE]
        for start in range(0, width, LANES):
            sent_ref[part, BLOCK : BLOCK + TILE, start : start + LANES] = own
    outs = []
    for chunk in range(chunks):
        for copy in copies[chunk]:
            copy.wait()
        mine = slice(chunk * step, (chunk + 1) * step)
        for part in range(chunk * step, (chunk + 1) * step):
            columns = slice(part * width, (part + 1) * width)
            sent_ref[part, 0:BLOCK, :] = (
                key_ref[:, columns].astype(jnp.float32) * value_ref[:, columns].astype(jnp.float32)
            ).astype(jnp.bfloat16)
        out = pltpu.make_async_copy(sent_ref.at[mine], sent_hbm.at[mine], left.at[chunk])
        out.start()
        outs.append(out)
    for out in outs:
        out.wait()


def conv_kernel(sources, *refs):
    got_refs, (conv_ref, taps, results) = refs[:sources], refs[sources : sources + 3]
    turned_refs = refs[sources + 3 :]
    halves = conv_ref.shape[2] // LANES
    for lag in range(LAGS):
        taps[lag] = got_refs[0][lag, BLOCK : BLOCK + TILE, 0:LANES].astype(jnp.float32)
    lane = lax.broadcasted_iota(jnp.int32, (BLOCK, LANES), 1)
    row = lax.broadcasted_iota(jnp.int32, (BLOCK, LANES), 0)
    causal = row >= lane

    @pl.loop(0, halves)
    def _(half):
        columns = pl.ds(pl.multiple_of(half * LANES, LANES), LANES)
        for got_ref, turned_ref in zip(got_refs, turned_refs):
            for block in range(LAGS):
                tile = got_ref[block, 0:BLOCK, columns]
                turned_ref[block] = pltpu.roll(tile, block * GROUP, 1) if block else tile
        for side in range(SIDE):
            holds = (lane // GROUP + (SIDE - side)) % SIDE
            sources_here = []
            for turned_ref in turned_refs:
                source = turned_ref[0]
                for block in range(1, LAGS):
                    source = jnp.where(holds == block, turned_ref[block], source)
                sources_here.append(source)
            before = jnp.zeros((BLOCK, LANES), jnp.float32)
            filters, shifted = [], []
            for lag in range(LAGS):
                own = taps[lag, pl.ds(half * SIDE + side, 1), :]
                turned = pltpu.roll(jnp.broadcast_to(own, (BLOCK, LANES)), 0, 1, stride=1, stride_axis=0)
                filters.append(jnp.where(causal, turned, before).astype(jnp.bfloat16))
                before = turned
                moved = [pltpu.roll(source, lag * GROUP, 1) if lag else source for source in sources_here]
                if lag:
                    carried = moved[1] if sources > 1 else jnp.zeros_like(moved[0])
                    moved[0] = jnp.where(holds >= lag, moved[0], carried)
                shifted.append(moved[0])
            total = jnp.dot(
                jnp.concatenate(filters, axis=1),
                jnp.concatenate(shifted, axis=0),
                preferred_element_type=jnp.float32,
            )
            results[half * SIDE + side] = total.astype(jnp.bfloat16)

    tall = 4 * TILE
    granule = lax.broadcasted_iota(jnp.int32, (tall, LANES), 1) // GROUP
    for half in range(halves):

        @pl.loop(0, BLOCK // tall)
        def _(step):
            rows = pl.ds(pl.multiple_of(step * tall, tall), tall)
            tiles = [results[half * SIDE + side, rows, :] for side in range(SIDE)]
            for block in range(LAGS):
                total = tiles[0]
                for side in range(1, SIDE):
                    total = jnp.where(granule == (side + block) % SIDE, tiles[side], total)
                turned = pltpu.roll(total, (SIDE - block) * GROUP, 1) if block else total
                conv_ref[block, rows, half * LANES : (half + 1) * LANES] = turned


def gate_kernel(parts, query_ref, key_ref, value_ref, conv_ref, skip_ref, gated_ref):
    width = conv_ref.shape[2]
    for part in range(parts):
        for start in range(0, width, LANES):
            columns = slice(part * width + start, part * width + start + LANES)
            mixed = (
                key_ref[:, columns].astype(jnp.float32) * value_ref[:, columns].astype(jnp.float32)
            ).astype(jnp.bfloat16).astype(jnp.float32)
            conv = conv_ref[part, :, start : start + LANES].astype(jnp.float32)
            summed = conv + skip_ref[:, columns] * mixed
            gated_ref[:, columns] = (query_ref[:, columns].astype(jnp.float32) * summed).astype(jnp.bfloat16)


def per_device(query, key, value, filter_taps, skip):
    rows, channels = query.shape
    parts = LAGS
    width = channels // parts
    count = lax.axis_size("ctx")
    windows = None
    if count > LAGS:
        windows = [list(range(first, first + LAGS)) for first in range(0, count, LAGS)]
        all_taps = lax.all_gather(filter_taps, "ctx", axis=0, tiled=True)
        filter_taps = lax.dynamic_slice_in_dim(all_taps, lax.axis_index("ctx") % LAGS * BLOCK, BLOCK, axis=0)
    sent = pl.pallas_call(
        lambda *refs: mix_kernel(parts, CHUNKS, *refs),
        out_shape=jax.ShapeDtypeStruct((parts, BLOCK + TILE, width), jnp.bfloat16),
        in_specs=[pl.BlockSpec(memory_space=pl.ANY)] * 3,
        out_specs=pl.BlockSpec(memory_space=pl.ANY),
        scratch_shapes=[
            pltpu.VMEM(key.shape, key.dtype),
            pltpu.VMEM(value.shape, value.dtype),
            pltpu.VMEM(filter_taps.shape, filter_taps.dtype),
            pltpu.VMEM((parts, BLOCK + TILE, width), jnp.bfloat16),
            pltpu.SemaphoreType.DMA((2 * CHUNKS + 1,)),
            pltpu.SemaphoreType.DMA((CHUNKS,)),
        ],
    )(key, value, filter_taps)
    got = [lax.all_to_all(sent, "ctx", 0, 0, tiled=True, axis_index_groups=windows)]
    if count > LAGS:
        onward = [(source, source + LAGS) for source in range(count - LAGS)]
        got.append(lax.ppermute(got[0], "ctx", onward))
    conv = pl.pallas_call(
        lambda *refs: conv_kernel(len(got), *refs),
        out_shape=jax.ShapeDtypeStruct((parts, BLOCK, width), jnp.bfloat16),
        scratch_shapes=[
            pltpu.VMEM((LAGS, TILE, LANES), jnp.float32),
            pltpu.VMEM((width // GROUP, BLOCK, LANES), jnp.bfloat16),
        ]
        + [pltpu.VMEM((LAGS, BLOCK, LANES), jnp.bfloat16)] * len(got),
        compiler_params=SMALL,
    )(*got)
    back = lax.all_to_all(conv, "ctx", 0, 0, tiled=True, axis_index_groups=windows)
    return pl.pallas_call(
        lambda *refs: gate_kernel(parts, *refs),
        out_shape=jax.ShapeDtypeStruct((rows, channels), jnp.bfloat16),
        compiler_params=SMALL,
    )(query, key, value, back, skip.reshape(1, channels))


def solution(mesh):
    placed = (P("ctx", "ch"), P("ctx", "ch"), P("ctx", "ch"), P("ctx", "ch"), P("ch"))
    return jax.shard_map(
        per_device, mesh=mesh, in_specs=placed, out_specs=P("ctx", "ch"), check_vma=False
    )
```

```python
import jax
import jax.numpy as jnp
from jax import lax
from jax.experimental import pallas as pl
from jax.experimental.pallas import tpu as pltpu
from jax.sharding import PartitionSpec as P

GROUP = 16
BLOCK = 128
LAGS = 8
LANES = 128
TILE = 16
SIDE = LANES // GROUP
ORDER = (4, 1, 5, 2, 6, 3, 7)
STEPS = (0,) + ORDER
CHUNKS = 2
SMALL = pltpu.CompilerParams(vmem_limit_bytes=16 * 1024 * 1024)


def partner(step):
    return (lax.axis_index("ctx") % LAGS) ^ step


def exchange(blocks):
    pairs = lambda step: [(source, source ^ step) for source in range(lax.axis_size("ctx"))]
    return [blocks[0]] + [lax.ppermute(block, "ctx", pairs(step)) for block, step in zip(blocks[1:], ORDER)]


def turned_back(block):
    return pltpu.roll(block, (SIDE - partner(0)) % SIDE * GROUP, 1)


def mix_kernel(key_hbm, value_hbm, taps_hbm, *refs):
    sent_refs, (key_ref, value_ref, taps_ref, mirrored_ref, arrived) = refs[:LAGS], refs[LAGS:]
    halves = sent_refs[0].shape[0] // BLOCK
    rows = BLOCK // CHUNKS
    taps_copy = pltpu.make_async_copy(taps_hbm, taps_ref, arrived.at[2 * CHUNKS])
    taps_copy.start()
    copies = []
    for chunk in range(CHUNKS):
        here = slice(chunk * rows, (chunk + 1) * rows)
        pair = [
            pltpu.make_async_copy(key_hbm.at[here], key_ref.at[here], arrived.at[2 * chunk]),
            pltpu.make_async_copy(value_hbm.at[here], value_ref.at[here], arrived.at[2 * chunk + 1]),
        ]
        for copy in pair:
            copy.start()
        copies.append(pair)
    tap = lax.broadcasted_iota(jnp.int32, (BLOCK, LANES), 0)
    place = lax.broadcasted_iota(jnp.int32, (BLOCK, LANES), 1)
    mirror = jnp.where((tap + place) % BLOCK == 0, 1.0, 0.0).astype(jnp.bfloat16)
    taps_copy.wait()
    mirrored_ref[...] = lax.dot_general(
        taps_ref[...], mirror, (((0,), (0,)), ((), ())), preferred_element_type=jnp.float32
    ).astype(jnp.bfloat16)
    for step, sent_ref in zip(STEPS, sent_refs):
        first = pl.multiple_of(partner(step) * TILE, TILE)
        sent_ref[halves * BLOCK : halves * BLOCK + TILE, :] = mirrored_ref[pl.ds(first, TILE), :]
    for chunk in range(CHUNKS):
        for copy in copies[chunk]:
            copy.wait()
        here = slice(chunk * rows, (chunk + 1) * rows)
        for step, sent_ref in zip(STEPS, sent_refs):
            for half in range(halves):
                columns = pl.ds(pl.multiple_of((partner(step) * halves + half) * LANES, LANES), LANES)
                mixed = (
                    key_ref[here, columns].astype(jnp.float32) * value_ref[here, columns].astype(jnp.float32)
                ).astype(jnp.bfloat16)
                there = slice(half * BLOCK + chunk * rows, half * BLOCK + (chunk + 1) * rows)
                sent_ref[there, :] = pltpu.roll(mixed, partner(0) * GROUP, 1)


def conv_kernel(sources, *refs):
    inputs = sources * LAGS
    got_refs = [refs[first : first + LAGS] for first in range(0, inputs, LAGS)]
    conv_refs = refs[inputs : inputs + LAGS]
    taps, results = refs[inputs + LAGS :]
    halves = conv_refs[0].shape[0] // BLOCK
    for step, got_ref in zip(STEPS, got_refs[0]):
        taps[partner(step)] = got_ref[halves * BLOCK : halves * BLOCK + TILE, :].astype(jnp.float32)
    lane = lax.broadcasted_iota(jnp.int32, (BLOCK, LANES), 1)
    row = lax.broadcasted_iota(jnp.int32, (BLOCK, LANES), 0)
    causal = row >= lane

    @pl.loop(0, halves)
    def _(half):
        rows = pl.ds(pl.multiple_of(half * BLOCK, BLOCK), BLOCK)
        for side in range(SIDE):
            holds = (lane // GROUP + (SIDE - side)) % SIDE
            sources_here = []
            for window in got_refs:
                source = window[0][rows, :]
                for step, got_ref in zip(ORDER, window[1:]):
                    source = jnp.where(holds == partner(step), got_ref[rows, :], source)
                sources_here.append(source)
            before = jnp.zeros((BLOCK, LANES), jnp.float32)
            filters, shifted = [], []
            for lag in range(LAGS):
                own = taps[lag, pl.ds(half * SIDE + side, 1), :]
                turned = pltpu.roll(jnp.broadcast_to(own, (BLOCK, LANES)), 0, 1, stride=1, stride_axis=0)
                filters.append(jnp.where(causal, turned, before).astype(jnp.bfloat16))
                before = turned
                moved = [pltpu.roll(source, lag * GROUP, 1) if lag else source for source in sources_here]
                if lag:
                    carried = moved[1] if sources > 1 else jnp.zeros_like(moved[0])
                    moved[0] = jnp.where(holds >= lag, moved[0], carried)
                shifted.append(moved[0])
            total = jnp.dot(
                jnp.concatenate(filters, axis=1),
                jnp.concatenate(shifted, axis=0),
                preferred_element_type=jnp.float32,
            )
            results[half * SIDE + side] = total.astype(jnp.bfloat16)

    tall = 4 * TILE
    granule = lax.broadcasted_iota(jnp.int32, (tall, LANES), 1) // GROUP
    for half in range(halves):

        @pl.loop(0, BLOCK // tall)
        def _(part):
            tiles = [results[half * SIDE + side, pl.ds(part * tall, tall), :] for side in range(SIDE)]
            for step, conv_ref in zip(STEPS, conv_refs):
                total = tiles[0]
                for side in range(1, SIDE):
                    total = jnp.where(granule == (side + partner(step)) % SIDE, tiles[side], total)
                conv_ref[pl.ds(half * BLOCK + part * tall, tall), :] = total


def gate_kernel(query_ref, skip_ref, *refs):
    sent_refs, conv_refs, (gated_hbm, gated_ref, left) = refs[:LAGS], refs[LAGS : 2 * LAGS], refs[2 * LAGS :]
    halves = conv_refs[0].shape[0] // BLOCK
    width = halves * LANES
    copies = []
    for index, step in enumerate(STEPS):
        for half in range(halves):
            columns = pl.ds(pl.multiple_of((partner(step) * halves + half) * LANES, LANES), LANES)
            rows = slice(half * BLOCK, (half + 1) * BLOCK)
            mixed = turned_back(sent_refs[index][rows, :]).astype(jnp.float32)
            conv = turned_back(conv_refs[index][rows, :]).astype(jnp.float32)
            summed = conv + skip_ref[:, columns] * mixed
            gated_ref[:, columns] = (query_ref[:, columns].astype(jnp.float32) * summed).astype(jnp.bfloat16)
        columns = pl.ds(pl.multiple_of(partner(step) * width, width), width)
        copy = pltpu.make_async_copy(gated_ref.at[:, columns], gated_hbm.at[:, columns], left.at[index])
        copy.start()
        copies.append(copy)
    for copy in copies:
        copy.wait()


def per_device(query, key, value, filter_taps, skip):
    rows, channels = query.shape
    halves = channels // LAGS // LANES
    count = lax.axis_size("ctx")
    if count > LAGS:
        all_taps = lax.all_gather(filter_taps, "ctx", axis=0, tiled=True)
        first_tap = lax.axis_index("ctx") % LAGS * BLOCK
        filter_taps = lax.dynamic_slice_in_dim(all_taps, first_tap, BLOCK, axis=0)
    in_hbm = [pltpu.with_memory_space_constraint(array, pltpu.HBM) for array in (key, value, filter_taps)]
    sent = pl.pallas_call(
        mix_kernel,
        out_shape=[jax.ShapeDtypeStruct((halves * BLOCK + TILE, LANES), jnp.bfloat16)] * LAGS,
        in_specs=[pl.BlockSpec(memory_space=pl.ANY)] * 3,
        scratch_shapes=[
            pltpu.VMEM(key.shape, key.dtype),
            pltpu.VMEM(value.shape, value.dtype),
            pltpu.VMEM(filter_taps.shape, filter_taps.dtype),
            pltpu.VMEM((LANES, BLOCK), jnp.bfloat16),
            pltpu.SemaphoreType.DMA((2 * CHUNKS + 1,)),
        ],
        compiler_params=SMALL,
    )(*in_hbm)
    got = exchange(sent)
    sources = 1
    if count > LAGS:
        sources = 2
        onward = [(source, source + LAGS) for source in range(count - LAGS)]
        got = got + [lax.ppermute(block, "ctx", onward) for block in got]
    conv = pl.pallas_call(
        lambda *refs: conv_kernel(sources, *refs),
        out_shape=[jax.ShapeDtypeStruct((halves * BLOCK, LANES), jnp.bfloat16)] * LAGS,
        scratch_shapes=[
            pltpu.VMEM((LAGS, TILE, LANES), jnp.float32),
            pltpu.VMEM((halves * SIDE, BLOCK, LANES), jnp.bfloat16),
        ],
        compiler_params=SMALL,
    )(*got)
    back = exchange(conv)
    whole = pl.BlockSpec(memory_space=pltpu.VMEM)
    return pl.pallas_call(
        gate_kernel,
        out_shape=jax.ShapeDtypeStruct((rows, channels), jnp.bfloat16),
        in_specs=[whole] * (2 + 2 * LAGS),
        out_specs=pl.BlockSpec(memory_space=pl.ANY),
        scratch_shapes=[pltpu.VMEM((rows, channels), jnp.bfloat16), pltpu.SemaphoreType.DMA((LAGS,))],
        compiler_params=SMALL,
    )(query, skip.reshape(1, channels), *sent, *back)


def solution(mesh):
    placed = (P("ctx", "ch"), P("ctx", "ch"), P("ctx", "ch"), P("ctx", "ch"), P("ch"))
    return jax.shard_map(
        per_device, mesh=mesh, in_specs=placed, out_specs=P("ctx", "ch"), check_vma=False
    )
```

```python
import jax
import jax.numpy as jnp
from jax import lax
from jax.experimental import pallas as pl
from jax.experimental.pallas import tpu as pltpu
from jax.sharding import PartitionSpec as P

GROUP = 16
BLOCK = 128
LAGS = 8
LANES = 128
TILE = 16
SIDE = LANES // GROUP
GATHER = ((6, 1, 4, 2, 5, 3, 7), (6, 1, 4, 2, 5, 3, 7))
RETURN = ((4, 1, 5, 2, 6, 3, 7), (4, 1, 5, 2, 6, 3, 7))
CHUNKS = 2
EARLY = 7
SMALL = pltpu.CompilerParams(vmem_limit_bytes=16 * 1024 * 1024)


def place():
    return lax.axis_index("ctx") % LAGS


def partners(orders):
    core = lax.axis_index("ch") % 2
    return [place()] + [place() ^ jnp.where(core == 0, first, second) for first, second in zip(*orders)]


def exchange(blocks, orders):
    size = lax.axis_size("ch")
    devices = range(lax.axis_size("ctx") * size)
    got = [blocks[0]]
    for block, steps in zip(blocks[1:], zip(*orders)):
        pairs = [(one, (one // size ^ steps[one % size % 2]) * size + one % size) for one in devices]
        got.append(lax.ppermute(block, ("ctx", "ch"), pairs))
    return got


def turned_back(block):
    return pltpu.roll(block, (SIDE - place()) % SIDE * GROUP, 1)


def mix_kernel(key_hbm, value_hbm, taps_hbm, *refs):
    sent_refs, (mixed_ref, key_ref, value_ref, taps_ref, mirrored_ref, arrived) = refs[:LAGS], refs[LAGS:]
    halves = sent_refs[0].shape[0] // BLOCK
    rows = BLOCK // CHUNKS
    taps_copy = pltpu.make_async_copy(taps_hbm, taps_ref, arrived.at[2 * CHUNKS])
    taps_copy.start()
    copies = []
    for chunk in range(CHUNKS):
        here = slice(chunk * rows, (chunk + 1) * rows)
        pair = [
            pltpu.make_async_copy(key_hbm.at[here], key_ref.at[here], arrived.at[2 * chunk]),
            pltpu.make_async_copy(value_hbm.at[here], value_ref.at[here], arrived.at[2 * chunk + 1]),
        ]
        for copy in pair:
            copy.start()
        copies.append(pair)
    tap = lax.broadcasted_iota(jnp.int32, (BLOCK, LANES), 0)
    column = lax.broadcasted_iota(jnp.int32, (BLOCK, LANES), 1)
    mirror = jnp.where((tap + column) % BLOCK == 0, 1.0, 0.0).astype(jnp.bfloat16)
    taps_copy.wait()
    mirrored_ref[...] = lax.dot_general(
        taps_ref[...], mirror, (((0,), (0,)), ((), ())), preferred_element_type=jnp.float32
    ).astype(jnp.bfloat16)
    for partner, sent_ref in zip(partners(GATHER), sent_refs):
        first = pl.multiple_of(partner * TILE, TILE)
        sent_ref[halves * BLOCK : halves * BLOCK + TILE, :] = mirrored_ref[pl.ds(first, TILE), :]
    for chunk in range(CHUNKS):
        for copy in copies[chunk]:
            copy.wait()
        here = slice(chunk * rows, (chunk + 1) * rows)
        for partner, sent_ref in zip(partners(GATHER), sent_refs):
            for half in range(halves):
                columns = pl.ds(pl.multiple_of((partner * halves + half) * LANES, LANES), LANES)
                mixed = (
                    key_ref[here, columns].astype(jnp.float32) * value_ref[here, columns].astype(jnp.float32)
                ).astype(jnp.bfloat16)
                mixed_ref[here, columns] = mixed
                there = slice(half * BLOCK + chunk * rows, half * BLOCK + (chunk + 1) * rows)
                sent_ref[there, :] = pltpu.roll(mixed, place() * GROUP, 1)


def add_circulants(where, got_refs, circulants, taps):
    rows = got_refs[0].shape[0]
    for index, got_ref in enumerate(got_refs):
        taps[index] = got_ref[rows - TILE : rows, :].astype(jnp.float32)

    @pl.loop(0, TILE, unroll=8)
    def _(group):
        for index, partner in enumerate(where):
            own = jnp.broadcast_to(taps[index, pl.ds(group, 1), :], (BLOCK, LANES))
            circulants[partner, group] = pltpu.roll(own, 0, 1, stride=1, stride_axis=0).astype(jnp.bfloat16)


def early_kernel(*refs):
    *got_refs, circulants, taps = refs
    add_circulants(partners(GATHER)[:EARLY], got_refs, circulants, taps)


def conv_kernel(sources, *refs):
    inputs = sources * LAGS
    got_refs = [refs[first : first + LAGS] for first in range(0, inputs, LAGS)]
    _, *conv_refs, circulants, taps, results = refs[inputs:]
    halves = conv_refs[0].shape[0] // BLOCK
    add_circulants(partners(GATHER)[EARLY:], got_refs[0][EARLY:], circulants, taps)
    lane = lax.broadcasted_iota(jnp.int32, (BLOCK, LANES), 1)
    row = lax.broadcasted_iota(jnp.int32, (BLOCK, LANES), 0)
    causal = row.astype(jnp.int16) >= lane.astype(jnp.int16)
    granule = lane // GROUP
    for group in range(halves * SIDE):
        half, side = divmod(group, SIDE)
        rows = slice(half * BLOCK, (half + 1) * BLOCK)
        holds = (granule + (SIDE - side)) % SIDE
        sources_here = []
        for window in got_refs:
            source = window[0][rows, :]
            for partner, got_ref in zip(partners(GATHER)[1:], window[1:]):
                source = jnp.where(holds == partner, got_ref[rows, :], source)
            sources_here.append(source)
        before = jnp.zeros((BLOCK, LANES), jnp.bfloat16)
        filters, shifted = [], []
        for lag in range(LAGS):
            turned = circulants[lag, group]
            filters.append(jnp.where(causal, turned, before))
            before = turned
            moved = [pltpu.roll(source, lag * GROUP, 1) if lag else source for source in sources_here]
            if lag:
                carried = moved[1] if sources > 1 else jnp.zeros_like(moved[0])
                moved[0] = jnp.where(holds >= lag, moved[0], carried)
            shifted.append(moved[0])
        total = jnp.dot(
            jnp.concatenate(filters, axis=1),
            jnp.concatenate(shifted, axis=0),
            preferred_element_type=jnp.float32,
        )
        results[group] = total.astype(jnp.bfloat16)
    for half in range(halves):
        tiles = [results[half * SIDE + side] for side in range(SIDE)]
        for partner, conv_ref in zip(partners(RETURN), conv_refs):
            total = tiles[0]
            for side in range(1, SIDE):
                total = jnp.where(granule == (side + partner) % SIDE, tiles[side], total)
            conv_ref[half * BLOCK : (half + 1) * BLOCK, :] = total


def gate_kernel(query_ref, skip_ref, mixed_ref, *refs):
    conv_refs, (gated_hbm, gated_ref, left) = refs[:LAGS], refs[LAGS:]
    halves = conv_refs[0].shape[0] // BLOCK
    width = halves * LANES
    copies = []
    for index, partner in enumerate(partners(RETURN)):
        for half in range(halves):
            columns = pl.ds(pl.multiple_of((partner * halves + half) * LANES, LANES), LANES)
            rows = slice(half * BLOCK, (half + 1) * BLOCK)
            mixed = mixed_ref[:, columns].astype(jnp.float32)
            conv = turned_back(conv_refs[index][rows, :]).astype(jnp.float32)
            summed = conv + skip_ref[:, columns] * mixed
            gated_ref[:, columns] = (query_ref[:, columns].astype(jnp.float32) * summed).astype(jnp.bfloat16)
        columns = pl.ds(pl.multiple_of(partner * width, width), width)
        copy = pltpu.make_async_copy(gated_ref.at[:, columns], gated_hbm.at[:, columns], left.at[index])
        copy.start()
        copies.append(copy)
    for copy in copies:
        copy.wait()


def per_device(query, key, value, filter_taps, skip):
    rows, channels = query.shape
    halves = channels // LAGS // LANES
    count = lax.axis_size("ctx")
    if count > LAGS:
        all_taps = lax.all_gather(filter_taps, "ctx", axis=0, tiled=True)
        first_tap = lax.axis_index("ctx") % LAGS * BLOCK
        filter_taps = lax.dynamic_slice_in_dim(all_taps, first_tap, BLOCK, axis=0)
    in_hbm = [pltpu.with_memory_space_constraint(array, pltpu.HBM) for array in (key, value, filter_taps)]
    *sent, mixed = pl.pallas_call(
        mix_kernel,
        out_shape=[jax.ShapeDtypeStruct((halves * BLOCK + TILE, LANES), jnp.bfloat16)] * LAGS
        + [jax.ShapeDtypeStruct(key.shape, jnp.bfloat16)],
        in_specs=[pl.BlockSpec(memory_space=pl.ANY)] * 3,
        scratch_shapes=[
            pltpu.VMEM(key.shape, key.dtype),
            pltpu.VMEM(value.shape, value.dtype),
            pltpu.VMEM(filter_taps.shape, filter_taps.dtype),
            pltpu.VMEM((LANES, BLOCK), jnp.bfloat16),
            pltpu.SemaphoreType.DMA((2 * CHUNKS + 1,)),
        ],
        compiler_params=SMALL,
    )(*in_hbm)
    got = exchange(sent, GATHER)
    sources = 1
    if count > LAGS:
        sources = 2
        onward = [(source, source + LAGS) for source in range(count - LAGS)]
        got = got + [lax.ppermute(block, "ctx", onward) for block in got]
    whole = pl.BlockSpec(memory_space=pltpu.VMEM)
    every = jax.ShapeDtypeStruct((LAGS, TILE, BLOCK, LANES), jnp.bfloat16)
    circulants = pl.pallas_call(
        early_kernel,
        out_shape=every,
        in_specs=[whole] * EARLY,
        out_specs=whole,
        scratch_shapes=[pltpu.VMEM((EARLY, TILE, LANES), jnp.float32)],
        cost_estimate=pl.CostEstimate(flops=0, bytes_accessed=8 * 1024 * 1024, transcendentals=0),
        compiler_params=SMALL,
    )(*got[:EARLY])
    *conv, _ = pl.pallas_call(
        lambda *refs: conv_kernel(sources, *refs),
        out_shape=[jax.ShapeDtypeStruct((halves * BLOCK, LANES), jnp.bfloat16)] * LAGS + [every],
        in_specs=[whole] * (len(got) + 1),
        out_specs=[whole] * (LAGS + 1),
        scratch_shapes=[
            pltpu.VMEM((LAGS - EARLY, TILE, LANES), jnp.float32),
            pltpu.VMEM((halves * SIDE, BLOCK, LANES), jnp.bfloat16),
        ],
        input_output_aliases={len(got): LAGS},
        compiler_params=SMALL,
    )(*got, circulants)
    back = exchange(conv, RETURN)
    return pl.pallas_call(
        gate_kernel,
        out_shape=jax.ShapeDtypeStruct((rows, channels), jnp.bfloat16),
        in_specs=[whole] * (3 + LAGS),
        out_specs=pl.BlockSpec(memory_space=pl.ANY),
        scratch_shapes=[pltpu.VMEM((rows, channels), jnp.bfloat16), pltpu.SemaphoreType.DMA((LAGS,))],
        compiler_params=SMALL,
    )(query, skip.reshape(1, channels), mixed, *back)


def solution(mesh):
    placed = (P("ctx", "ch"), P("ctx", "ch"), P("ctx", "ch"), P("ctx", "ch"), P("ch"))
    return jax.shard_map(
        per_device, mesh=mesh, in_specs=placed, out_specs=P("ctx", "ch"), check_vma=False
    )
```

```python
import functools

import jax
import jax.numpy as jnp
from jax import lax
from jax.experimental import pallas as pl
from jax.experimental.pallas import tpu as pltpu
from jax.sharding import PartitionSpec as P

GROUP = 16
BLOCK = 128
LAGS = 8
LANES = 128
TILE = 16
SIDE = LANES // GROUP
GATHER = ((6, 2, 4, 1, 5, 3, 7), (6, 2, 4, 1, 5, 3, 7))
RETURN = ((4, 1, 5, 2, 6, 3, 7), (4, 1, 5, 2, 6, 3, 7))
CHUNKS = 2
EARLY = 7
AHEAD = 2
FIRST = 7
SMALL = pltpu.CompilerParams(vmem_limit_bytes=16 * 1024 * 1024)


def place():
    return lax.axis_index("ctx") % LAGS


def partners(orders):
    core = lax.axis_index("ch") % 2
    return [place()] + [place() ^ jnp.where(core == 0, first, second) for first, second in zip(*orders)]


def exchange(blocks, orders):
    size = lax.axis_size("ch")
    devices = range(lax.axis_size("ctx") * size)
    got = [blocks[0]]
    for block, steps in zip(blocks[1:], zip(*orders)):
        pairs = [(one, (one // size ^ steps[one % size % 2]) * size + one % size) for one in devices]
        got.append(lax.ppermute(block, ("ctx", "ch"), pairs))
    return got


def turned_back(block):
    return pltpu.roll(block, (SIDE - place()) % SIDE * GROUP, 1)


def mix_kernel(key_hbm, value_hbm, taps_hbm, *refs):
    sent_refs, (mixed_ref, key_ref, value_ref, taps_ref, mirrored_ref, arrived) = refs[:LAGS], refs[LAGS:]
    halves = sent_refs[0].shape[0] // BLOCK
    rows = BLOCK // CHUNKS
    taps_copy = pltpu.make_async_copy(taps_hbm, taps_ref, arrived.at[2 * CHUNKS])
    taps_copy.start()
    copies = []
    for chunk in range(CHUNKS):
        here = slice(chunk * rows, (chunk + 1) * rows)
        pair = [
            pltpu.make_async_copy(key_hbm.at[here], key_ref.at[here], arrived.at[2 * chunk]),
            pltpu.make_async_copy(value_hbm.at[here], value_ref.at[here], arrived.at[2 * chunk + 1]),
        ]
        for copy in pair:
            copy.start()
        copies.append(pair)
    tap = lax.broadcasted_iota(jnp.int32, (BLOCK, LANES), 0)
    column = lax.broadcasted_iota(jnp.int32, (BLOCK, LANES), 1)
    mirror = jnp.where((tap + column) % BLOCK == 0, 1.0, 0.0).astype(jnp.bfloat16)
    taps_copy.wait()
    mirrored_ref[...] = lax.dot_general(
        taps_ref[...], mirror, (((0,), (0,)), ((), ())), preferred_element_type=jnp.float32
    ).astype(jnp.bfloat16)
    for partner, sent_ref in zip(partners(GATHER), sent_refs):
        first = pl.multiple_of(partner * TILE, TILE)
        sent_ref[halves * BLOCK : halves * BLOCK + TILE, :] = mirrored_ref[pl.ds(first, TILE), :]
    for chunk in range(CHUNKS):
        for copy in copies[chunk]:
            copy.wait()
        here = slice(chunk * rows, (chunk + 1) * rows)
        for partner, sent_ref in zip(partners(GATHER), sent_refs):
            for half in range(halves):
                columns = pl.ds(pl.multiple_of((partner * halves + half) * LANES, LANES), LANES)
                mixed = (
                    key_ref[here, columns].astype(jnp.float32) * value_ref[here, columns].astype(jnp.float32)
                ).astype(jnp.bfloat16)
                mixed_ref[here, columns] = mixed
                there = slice(half * BLOCK + chunk * rows, half * BLOCK + (chunk + 1) * rows)
                sent_ref[there, :] = pltpu.roll(mixed, place() * GROUP, 1)


def circulant(row):
    return pltpu.roll(jnp.broadcast_to(row, (BLOCK, LANES)), 0, 1, stride=1, stride_axis=0).astype(jnp.bfloat16)


def early_kernel(*refs):
    *got_refs, circulants, taps = refs
    rows = got_refs[0].shape[0]
    for index, got_ref in enumerate(got_refs):
        taps[index] = got_ref[rows - TILE : rows, :].astype(jnp.float32)

    @pl.loop(0, TILE, unroll=8)
    def _(group):
        for index, partner in enumerate(partners(GATHER)[:EARLY]):
            circulants[partner, group] = circulant(taps[index, pl.ds(group, 1), :])


def conv_kernel(sources, *refs):
    inputs = sources * LAGS
    got_refs = [refs[first : first + LAGS] for first in range(0, inputs, LAGS)]
    _, *conv_refs, circulants, taps, results = refs[inputs:]
    halves = conv_refs[0].shape[0] // BLOCK
    late = list(zip(partners(GATHER), got_refs[0]))[EARLY:]
    for index, (_, got_ref) in enumerate(late):
        taps[index] = got_ref[halves * BLOCK : halves * BLOCK + TILE, :].astype(jnp.float32)

    def add_late(group):
        for index, (partner, _) in enumerate(late):
            circulants[partner, group] = circulant(taps[index, group : group + 1, :])

    for group in range(AHEAD):
        add_late(group)
    lane = lax.broadcasted_iota(jnp.int32, (BLOCK, LANES), 1)
    row = lax.broadcasted_iota(jnp.int32, (BLOCK, LANES), 0)
    causal = row.astype(jnp.int16) >= lane.astype(jnp.int16)
    granule = lane // GROUP
    for group in range(halves * SIDE):
        if group + AHEAD < halves * SIDE:
            add_late(group + AHEAD)
        half, side = divmod(group, SIDE)
        rows = slice(half * BLOCK, (half + 1) * BLOCK)
        holds = (granule + (SIDE - side)) % SIDE
        sources_here = []
        for window in got_refs:
            source = window[0][rows, :]
            for partner, got_ref in zip(partners(GATHER)[1:], window[1:]):
                source = jnp.where(holds == partner, got_ref[rows, :], source)
            sources_here.append(source)
        before = jnp.zeros((BLOCK, LANES), jnp.bfloat16)
        filters, shifted = [], []
        for lag in range(LAGS):
            turned = circulants[lag, group]
            filters.append(jnp.where(causal, turned, before))
            before = turned
            moved = [pltpu.roll(source, lag * GROUP, 1) if lag else source for source in sources_here]
            if lag:
                carried = moved[1] if sources > 1 else jnp.zeros_like(moved[0])
                moved[0] = jnp.where(holds >= lag, moved[0], carried)
            shifted.append(moved[0])
        total = jnp.dot(
            jnp.concatenate(filters, axis=1),
            jnp.concatenate(shifted, axis=0),
            preferred_element_type=jnp.float32,
        )
        results[group] = total.astype(jnp.bfloat16)
    for half in range(halves):
        tiles = [results[half * SIDE + side] for side in range(SIDE)]
        for partner, conv_ref in zip(partners(RETURN), conv_refs):
            total = tiles[0]
            for side in range(1, SIDE):
                total = jnp.where(granule == (side + partner) % SIDE, tiles[side], total)
            conv_ref[half * BLOCK : (half + 1) * BLOCK, :] = total


def gate_kernel(rounds, query_ref, skip_ref, mixed_ref, *refs):
    conv_refs, (gated_hbm, gated_ref, left) = refs[: rounds.stop - rounds.start], refs[-3:]
    halves = conv_refs[0].shape[0] // BLOCK
    width = halves * LANES
    copies = []
    for index, partner in enumerate(partners(RETURN)[rounds]):
        for half in range(halves):
            columns = pl.ds(pl.multiple_of((partner * halves + half) * LANES, LANES), LANES)
            rows = slice(half * BLOCK, (half + 1) * BLOCK)
            mixed = mixed_ref[:, columns].astype(jnp.float32)
            conv = turned_back(conv_refs[index][rows, :]).astype(jnp.float32)
            summed = conv + skip_ref[:, columns] * mixed
            gated_ref[:, columns] = (query_ref[:, columns].astype(jnp.float32) * summed).astype(jnp.bfloat16)
        columns = pl.ds(pl.multiple_of(partner * width, width), width)
        copy = pltpu.make_async_copy(gated_ref.at[:, columns], gated_hbm.at[:, columns], left.at[index])
        copy.start()
        copies.append(copy)
    for copy in copies:
        copy.wait()


def per_device(query, key, value, filter_taps, skip):
    rows, channels = query.shape
    halves = channels // LAGS // LANES
    count = lax.axis_size("ctx")
    if count > LAGS:
        all_taps = lax.all_gather(filter_taps, "ctx", axis=0, tiled=True)
        first_tap = lax.axis_index("ctx") % LAGS * BLOCK
        filter_taps = lax.dynamic_slice_in_dim(all_taps, first_tap, BLOCK, axis=0)
    in_hbm = [pltpu.with_memory_space_constraint(array, pltpu.HBM) for array in (key, value, filter_taps)]
    *sent, mixed = pl.pallas_call(
        mix_kernel,
        out_shape=[jax.ShapeDtypeStruct((halves * BLOCK + TILE, LANES), jnp.bfloat16)] * LAGS
        + [jax.ShapeDtypeStruct(key.shape, jnp.bfloat16)],
        in_specs=[pl.BlockSpec(memory_space=pl.ANY)] * 3,
        scratch_shapes=[
            pltpu.VMEM(key.shape, key.dtype),
            pltpu.VMEM(value.shape, value.dtype),
            pltpu.VMEM(filter_taps.shape, filter_taps.dtype),
            pltpu.VMEM((LANES, BLOCK), jnp.bfloat16),
            pltpu.SemaphoreType.DMA((2 * CHUNKS + 1,)),
        ],
        compiler_params=SMALL,
    )(*in_hbm)
    got = exchange(sent, GATHER)
    sources = 1
    if count > LAGS:
        sources = 2
        onward = [(source, source + LAGS) for source in range(count - LAGS)]
        got = got + [lax.ppermute(block, "ctx", onward) for block in got]
    whole = pl.BlockSpec(memory_space=pltpu.VMEM)
    every = jax.ShapeDtypeStruct((LAGS, TILE, BLOCK, LANES), jnp.bfloat16)
    circulants = pl.pallas_call(
        early_kernel,
        out_shape=every,
        in_specs=[whole] * EARLY,
        out_specs=whole,
        scratch_shapes=[pltpu.VMEM((EARLY, TILE, LANES), jnp.float32)],
        cost_estimate=pl.CostEstimate(flops=0, bytes_accessed=8 * 1024 * 1024, transcendentals=0),
        compiler_params=SMALL,
    )(*got[:EARLY])
    *conv, _ = pl.pallas_call(
        lambda *refs: conv_kernel(sources, *refs),
        out_shape=[jax.ShapeDtypeStruct((halves * BLOCK, LANES), jnp.bfloat16)] * LAGS + [every],
        in_specs=[whole] * (len(got) + 1),
        out_specs=[whole] * (LAGS + 1),
        scratch_shapes=[
            pltpu.VMEM((LAGS - EARLY, TILE, LANES), jnp.float32),
            pltpu.VMEM((halves * SIDE, BLOCK, LANES), jnp.bfloat16),
        ],
        input_output_aliases={len(got): LAGS},
        compiler_params=SMALL,
    )(*got, circulants)
    back = exchange(conv, RETURN)
    gated = None
    for rounds in (slice(0, FIRST), slice(FIRST, LAGS)):
        size = rounds.stop - rounds.start
        inputs = [query, skip.reshape(1, channels), mixed, *back[rounds]]
        specs = [whole] * len(inputs)
        if gated is not None:
            inputs.append(gated)
            specs.append(pl.BlockSpec(memory_space=pl.ANY))
        gated = pl.pallas_call(
            functools.partial(gate_kernel, rounds),
            out_shape=jax.ShapeDtypeStruct((rows, channels), jnp.bfloat16),
            in_specs=specs,
            out_specs=pl.BlockSpec(memory_space=pl.ANY),
            scratch_shapes=[pltpu.VMEM((rows, channels), jnp.bfloat16), pltpu.SemaphoreType.DMA((size,))],
            input_output_aliases={} if gated is None else {len(inputs) - 1: 0},
            compiler_params=SMALL,
        )(*inputs)
    return gated


def solution(mesh):
    placed = (P("ctx", "ch"), P("ctx", "ch"), P("ctx", "ch"), P("ctx", "ch"), P("ch"))
    return jax.shard_map(
        per_device, mesh=mesh, in_specs=placed, out_specs=P("ctx", "ch"), check_vma=False
    )
```

```python
import functools

import jax
import jax.numpy as jnp
from jax import lax
from jax.experimental import pallas as pl
from jax.experimental.pallas import tpu as pltpu
from jax.sharding import PartitionSpec as P

GROUP = 16
BLOCK = 128
LAGS = 8
LANES = 128
TILE = 16
SIDE = LANES // GROUP
GATHER = ((6, 2, 4, 3, 5, 1, 7), (6, 2, 4, 3, 5, 1, 7))
RETURN = ((4, 1, 5, 2, 6, 3, 7), (4, 1, 5, 2, 6, 3, 7))
CHUNKS = 2
EARLY = 7
AHEAD = 2
FIRST = 7
SMALL = pltpu.CompilerParams(vmem_limit_bytes=16 * 1024 * 1024)


def place():
    return lax.axis_index("ctx") % LAGS


def partners(orders):
    core = lax.axis_index("ch") % 2
    return [place()] + [place() ^ jnp.where(core == 0, first, second) for first, second in zip(*orders)]


def exchange(blocks, orders):
    size = lax.axis_size("ch")
    devices = range(lax.axis_size("ctx") * size)
    got = [blocks[0]]
    for block, steps in zip(blocks[1:], zip(*orders)):
        pairs = [(one, (one // size ^ steps[one % size % 2]) * size + one % size) for one in devices]
        got.append(lax.ppermute(block, ("ctx", "ch"), pairs))
    return got


def mix_kernel(key_hbm, value_hbm, taps_hbm, *refs):
    sent_refs, (mixed_ref, key_ref, value_ref, taps_ref, turned_ref, arrived) = refs[:LAGS], refs[LAGS:]
    halves = sent_refs[0].shape[0] // BLOCK
    width = halves * LANES
    taps_copy = pltpu.make_async_copy(taps_hbm, taps_ref, arrived.at[4])
    taps_copy.start()
    copies = []
    for index, first in enumerate((place() & 4 ^ 4, place() & 4)):
        columns = pl.ds(pl.multiple_of(first * width, width), 4 * width)
        pair = [
            pltpu.make_async_copy(key_hbm.at[:, columns], key_ref.at[:, columns], arrived.at[2 * index]),
            pltpu.make_async_copy(value_hbm.at[:, columns], value_ref.at[:, columns], arrived.at[2 * index + 1]),
        ]
        for copy in pair:
            copy.start()
        copies.append(pair)
    taps_copy.wait()
    turned_ref[...] = taps_ref[...].T
    parts = list(zip(partners(GATHER), sent_refs))
    for partner, sent_ref in parts:
        first = pl.multiple_of(partner * TILE, TILE)
        sent_ref[width : width + TILE, :] = turned_ref[pl.ds(first, TILE), :]
    steps = (0,) + GATHER[0]
    for pair, here in zip(copies, (True, False)):
        for copy in pair:
            copy.wait()
        for step, (partner, sent_ref) in zip(steps, parts):
            if (step >= 4) != here:
                continue
            for half in range(halves):
                columns = pl.ds(pl.multiple_of((partner * halves + half) * LANES, LANES), LANES)
                mixed = (
                    key_ref[:, columns].astype(jnp.float32) * value_ref[:, columns].astype(jnp.float32)
                ).astype(jnp.bfloat16)
                mixed_ref[:, columns] = mixed
                sent_ref[half * BLOCK : (half + 1) * BLOCK, :] = mixed.T


def circulant(row):
    return pltpu.roll(jnp.broadcast_to(row, (BLOCK, LANES)), 0, 1, stride=1, stride_axis=0).astype(jnp.bfloat16)


def early_kernel(*refs):
    *got_refs, circulants, blocks, taps = refs
    width = blocks.shape[1]
    for index, (partner, got_ref) in enumerate(zip(partners(GATHER), got_refs)):
        taps[index] = got_ref[width : width + TILE, :].astype(jnp.float32)
        blocks[partner] = got_ref[0:width, :]

    @pl.loop(0, TILE, unroll=8)
    def _(group):
        for index, partner in enumerate(partners(GATHER)[:EARLY]):
            circulants[partner, group] = circulant(taps[index, pl.ds(group, 1), :])


def conv_kernel(sources, *refs):
    late_ref, *earlier_refs = refs[: 1 + (sources - 1) * LAGS]
    *conv_refs, circulants, blocks, taps, results, earlier = refs[1 + (sources - 1) * LAGS + 2 :]
    width = blocks.shape[1]
    late = partners(GATHER)[EARLY]
    taps[...] = late_ref[width : width + TILE, :].astype(jnp.float32)
    blocks[late] = late_ref[0:width, :]
    for partner, earlier_ref in zip(partners(GATHER), earlier_refs):
        earlier[partner] = earlier_ref[0:width, :]

    def add_late(group):
        circulants[late, group] = circulant(taps[group : group + 1, :])

    for group in range(AHEAD):
        add_late(group)
    causal = lax.broadcasted_iota(jnp.int32, (BLOCK, LANES), 1).astype(jnp.int16) >= lax.broadcasted_iota(
        jnp.int32, (BLOCK, LANES), 0
    ).astype(jnp.int16)
    for group in range(TILE):
        if group + AHEAD < TILE:
            add_late(group + AHEAD)
        rows = slice(group * GROUP, (group + 1) * GROUP)
        before = jnp.zeros((BLOCK, LANES), jnp.bfloat16)
        filters, signals = [], []
        for lag in range(LAGS):
            turned = circulants[lag, group]
            filters.append(jnp.where(causal, turned, before))
            before = turned
            signal = [blocks[block, rows, :] for block in range(LAGS - lag)]
            if sources > 1:
                signal = [earlier[block, rows, :] for block in range(LAGS - lag, LAGS)] + signal
            elif lag:
                signal = [jnp.zeros((lag * GROUP, LANES), jnp.bfloat16)] + signal
            signals.append(jnp.concatenate(signal, axis=0))
        total = jnp.dot(
            jnp.concatenate(signals, axis=1),
            jnp.concatenate(filters, axis=0),
            preferred_element_type=jnp.float32,
        )
        results[group] = total.astype(jnp.bfloat16)
    for partner, conv_ref in zip(partners(RETURN), conv_refs):
        rows = pl.ds(pl.multiple_of(partner * GROUP, GROUP), GROUP)
        for group in range(TILE):
            conv_ref[group * GROUP : (group + 1) * GROUP, :] = results[group, rows, :]


def gate_kernel(rounds, query_ref, skip_ref, mixed_ref, *refs):
    conv_refs, (gated_hbm, gated_ref, left) = refs[: rounds.stop - rounds.start], refs[-3:]
    halves = conv_refs[0].shape[0] // BLOCK
    width = halves * LANES
    copies = []
    for index, partner in enumerate(partners(RETURN)[rounds]):
        for half in range(halves):
            columns = pl.ds(pl.multiple_of((partner * halves + half) * LANES, LANES), LANES)
            rows = slice(half * BLOCK, (half + 1) * BLOCK)
            mixed = mixed_ref[:, columns].astype(jnp.float32)
            conv = conv_refs[index][rows, :].T.astype(jnp.float32)
            summed = conv + skip_ref[:, columns] * mixed
            gated_ref[:, columns] = (query_ref[:, columns].astype(jnp.float32) * summed).astype(jnp.bfloat16)
        columns = pl.ds(pl.multiple_of(partner * width, width), width)
        copy = pltpu.make_async_copy(gated_ref.at[:, columns], gated_hbm.at[:, columns], left.at[index])
        copy.start()
        copies.append(copy)
    for copy in copies:
        copy.wait()


def per_device(query, key, value, filter_taps, skip):
    rows, channels = query.shape
    halves = channels // LAGS // LANES
    count = lax.axis_size("ctx")
    if count > LAGS:
        all_taps = lax.all_gather(filter_taps, "ctx", axis=0, tiled=True)
        first_tap = lax.axis_index("ctx") % LAGS * BLOCK
        filter_taps = lax.dynamic_slice_in_dim(all_taps, first_tap, BLOCK, axis=0)
    in_hbm = [pltpu.with_memory_space_constraint(array, pltpu.HBM) for array in (key, value, filter_taps)]
    whole = pl.BlockSpec(memory_space=pltpu.VMEM)
    *sent, mixed = pl.pallas_call(
        mix_kernel,
        out_shape=[jax.ShapeDtypeStruct((halves * BLOCK + TILE, LANES), jnp.bfloat16)] * LAGS
        + [jax.ShapeDtypeStruct(key.shape, jnp.bfloat16)],
        in_specs=[pl.BlockSpec(memory_space=pl.ANY)] * 3,
        out_specs=[whole] * (LAGS + 1),
        scratch_shapes=[
            pltpu.VMEM(key.shape, key.dtype),
            pltpu.VMEM(value.shape, value.dtype),
            pltpu.VMEM(filter_taps.shape, filter_taps.dtype),
            pltpu.VMEM((LANES, BLOCK), jnp.bfloat16),
            pltpu.SemaphoreType.DMA((5,)),
        ],
        compiler_params=SMALL,
    )(*in_hbm)
    got = exchange(sent, GATHER)
    sources = 1
    if count > LAGS:
        sources = 2
        onward = [(source, source + LAGS) for source in range(count - LAGS)]
        got = got + [lax.ppermute(block, "ctx", onward) for block in got]
    prepared = [
        jax.ShapeDtypeStruct((LAGS, TILE, BLOCK, LANES), jnp.bfloat16),
        jax.ShapeDtypeStruct((LAGS, halves * BLOCK, LANES), jnp.bfloat16),
    ]
    early = pl.pallas_call(
        early_kernel,
        out_shape=prepared,
        in_specs=[whole] * EARLY,
        out_specs=[whole] * 2,
        scratch_shapes=[pltpu.VMEM((EARLY, TILE, LANES), jnp.float32)],
        cost_estimate=pl.CostEstimate(flops=0, bytes_accessed=8 * 1024 * 1024, transcendentals=0),
        compiler_params=SMALL,
    )(*got[:EARLY])
    late = got[EARLY:]
    *conv, _, _ = pl.pallas_call(
        lambda *refs: conv_kernel(sources, *refs),
        out_shape=[jax.ShapeDtypeStruct((halves * BLOCK, LANES), jnp.bfloat16)] * LAGS + prepared,
        in_specs=[whole] * (len(late) + 2),
        out_specs=[whole] * (LAGS + 2),
        scratch_shapes=[
            pltpu.VMEM((TILE, LANES), jnp.float32),
            pltpu.VMEM((TILE, BLOCK, LANES), jnp.bfloat16),
            pltpu.VMEM((LAGS, halves * BLOCK, LANES), jnp.bfloat16),
        ],
        input_output_aliases={len(late): LAGS, len(late) + 1: LAGS + 1},
        compiler_params=SMALL,
    )(*late, *early)
    back = exchange(conv, RETURN)
    gated = None
    for rounds in (slice(0, FIRST), slice(FIRST, LAGS)):
        size = rounds.stop - rounds.start
        inputs = [query, skip.reshape(1, channels), mixed, *back[rounds]]
        specs = [whole] * len(inputs)
        if gated is not None:
            inputs.append(gated)
            specs.append(pl.BlockSpec(memory_space=pl.ANY))
        gated = pl.pallas_call(
            functools.partial(gate_kernel, rounds),
            out_shape=jax.ShapeDtypeStruct((rows, channels), jnp.bfloat16),
            in_specs=specs,
            out_specs=pl.BlockSpec(memory_space=pl.ANY),
            scratch_shapes=[pltpu.VMEM((rows, channels), jnp.bfloat16), pltpu.SemaphoreType.DMA((size,))],
            input_output_aliases={} if gated is None else {len(inputs) - 1: 0},
            compiler_params=SMALL,
        )(*inputs)
    return gated


def solution(mesh):
    placed = (P("ctx", "ch"), P("ctx", "ch"), P("ctx", "ch"), P("ctx", "ch"), P("ch"))
    return jax.shard_map(
        per_device, mesh=mesh, in_specs=placed, out_specs=P("ctx", "ch"), check_vma=False
    )
```

```python
import functools

import jax
import jax.numpy as jnp
from jax import lax
from jax.experimental import pallas as pl
from jax.experimental.pallas import tpu as pltpu
from jax.sharding import PartitionSpec as P

GROUP = 16
BLOCK = 128
LAGS = 8
LANES = 128
TILE = 16
SIDE = LANES // GROUP
GATHER = ((6, 1, 4, 2, 5, 3, 7), (6, 1, 4, 2, 5, 3, 7))
RETURN = ((4, 1, 5, 2, 6, 3, 7), (4, 1, 5, 2, 6, 3, 7))
CHUNKS = 2
EARLY = 7
AHEAD = 2
UNROLL = 8
FIRST = 7
SMALL = pltpu.CompilerParams(vmem_limit_bytes=16 * 1024 * 1024)


def place():
    return lax.axis_index("ctx") % LAGS


def partners(orders):
    core = lax.axis_index("ch") % 2
    return [place()] + [place() ^ jnp.where(core == 0, first, second) for first, second in zip(*orders)]


def exchange(blocks, orders):
    size = lax.axis_size("ch")
    devices = range(lax.axis_size("ctx") * size)
    got = [blocks[0]]
    for block, steps in zip(blocks[1:], zip(*orders)):
        pairs = [(one, (one // size ^ steps[one % size % 2]) * size + one % size) for one in devices]
        got.append(lax.ppermute(block, ("ctx", "ch"), pairs))
    return got


def later_lanes():
    lane = lax.broadcasted_iota(jnp.int32, (BLOCK, LANES), 1)
    row = lax.broadcasted_iota(jnp.int32, (BLOCK, LANES), 0)
    return lane.astype(jnp.int16) >= row.astype(jnp.int16)


def mix_kernel(key_hbm, value_hbm, taps_hbm, *refs):
    sent_refs, refs = refs[:LAGS], refs[LAGS:]
    mixed_ref, home_ref, key_ref, value_ref, taps_ref, turned_ref, home_taps, arrived = refs
    halves = sent_refs[0].shape[0] // BLOCK
    width = halves * LANES
    taps_copy = pltpu.make_async_copy(taps_hbm, taps_ref, arrived.at[4])
    taps_copy.start()
    copies = []
    for index, first in enumerate((place() & 4 ^ 4, place() & 4)):
        columns = pl.ds(pl.multiple_of(first * width, width), 4 * width)
        pair = [
            pltpu.make_async_copy(key_hbm.at[:, columns], key_ref.at[:, columns], arrived.at[2 * index]),
            pltpu.make_async_copy(value_hbm.at[:, columns], value_ref.at[:, columns], arrived.at[2 * index + 1]),
        ]
        for copy in pair:
            copy.start()
        copies.append(pair)
    taps_copy.wait()
    turned_ref[...] = taps_ref[...].T
    parts = list(zip(partners(GATHER), sent_refs))
    for partner, sent_ref in parts:
        first = pl.multiple_of(partner * TILE, TILE)
        sent_ref[width : width + TILE, :] = turned_ref[pl.ds(first, TILE), :]
    steps = (0,) + GATHER[0]
    for pair, here in zip(copies, (True, False)):
        for copy in pair:
            copy.wait()
        for step, (partner, sent_ref) in zip(steps, parts):
            if (step >= 4) != here:
                continue
            for half in range(halves):
                columns = pl.ds(pl.multiple_of((partner * halves + half) * LANES, LANES), LANES)
                mixed = (
                    key_ref[:, columns].astype(jnp.float32) * value_ref[:, columns].astype(jnp.float32)
                ).astype(jnp.bfloat16)
                mixed_ref[:, columns] = mixed
                sent_ref[half * BLOCK : (half + 1) * BLOCK, :] = mixed.T

    @pl.when(lax.axis_index("ctx") == 0)
    def _():
        home_taps[...] = turned_ref[...].astype(jnp.float32)
        causal = later_lanes()
        for partner, sent_ref in parts:

            @pl.loop(0, TILE // 2, unroll=UNROLL)
            def _(pair):
                first = partner * TILE + 2 * pair
                rows = [circulant(home_taps[pl.ds(first + index, 1), :]) for index in range(2)]
                filters = [jnp.where(causal, row, jnp.zeros_like(row)) for row in rows]
                both = sent_ref[pl.ds(pl.multiple_of(2 * pair * GROUP, 2 * GROUP), 2 * GROUP), :]
                nothing = jnp.zeros((GROUP, LANES), jnp.bfloat16)
                signal = jnp.concatenate(
                    [
                        jnp.concatenate([both[0:GROUP], nothing], axis=0),
                        jnp.concatenate([nothing, both[GROUP : 2 * GROUP]], axis=0),
                    ],
                    axis=1,
                )
                total = jnp.dot(signal, jnp.concatenate(filters, axis=0), preferred_element_type=jnp.float32)
                there = pl.ds(pl.multiple_of(first * GROUP, 2 * GROUP), 2 * GROUP)
                home_ref[there, :] = total.astype(jnp.bfloat16)


def circulant(row):
    return pltpu.roll(jnp.broadcast_to(row, (BLOCK, LANES)), 0, 1, stride=1, stride_axis=0).astype(jnp.bfloat16)


def early_kernel(*refs):
    *got_refs, circulants, blocks, taps = refs
    width = blocks.shape[1]
    for index, (partner, got_ref) in enumerate(zip(partners(GATHER), got_refs)):
        taps[index] = got_ref[width : width + TILE, :].astype(jnp.float32)
        blocks[partner] = got_ref[0:width, :]

    @pl.loop(0, TILE, unroll=8)
    def _(group):
        for index, partner in enumerate(partners(GATHER)[:EARLY]):
            circulants[partner, group] = circulant(taps[index, pl.ds(group, 1), :])


def conv_kernel(sources, *refs):
    late_ref, *earlier_refs = refs[: 1 + (sources - 1) * LAGS]
    *conv_refs, circulants, blocks, taps, results, earlier = refs[1 + (sources - 1) * LAGS + 2 :]
    width = blocks.shape[1]
    late = partners(GATHER)[EARLY]
    taps[...] = late_ref[width : width + TILE, :].astype(jnp.float32)
    blocks[late] = late_ref[0:width, :]
    for partner, earlier_ref in zip(partners(GATHER), earlier_refs):
        earlier[partner] = earlier_ref[0:width, :]

    def add_late(group):
        circulants[late, group] = circulant(taps[group : group + 1, :])

    for group in range(AHEAD):
        add_late(group)
    causal = later_lanes()
    for group in range(TILE):
        if group + AHEAD < TILE:
            add_late(group + AHEAD)
        rows = slice(group * GROUP, (group + 1) * GROUP)
        before = jnp.zeros((BLOCK, LANES), jnp.bfloat16)
        filters, signals = [], []
        for lag in range(LAGS):
            turned = circulants[lag, group]
            filters.append(jnp.where(causal, turned, before))
            before = turned
            signal = [blocks[block, rows, :] for block in range(LAGS - lag)]
            if sources > 1:
                signal = [earlier[block, rows, :] for block in range(LAGS - lag, LAGS)] + signal
            elif lag:
                signal = [jnp.zeros((lag * GROUP, LANES), jnp.bfloat16)] + signal
            signals.append(jnp.concatenate(signal, axis=0))
        total = jnp.dot(
            jnp.concatenate(signals, axis=1),
            jnp.concatenate(filters, axis=0),
            preferred_element_type=jnp.float32,
        )
        results[group] = total.astype(jnp.bfloat16)
    for partner, conv_ref in zip(partners(RETURN), conv_refs):
        rows = pl.ds(pl.multiple_of(partner * GROUP, GROUP), GROUP)
        for group in range(TILE):
            conv_ref[group * GROUP : (group + 1) * GROUP, :] = results[group, rows, :]


def gate_parts(numbers, convs, query_ref, skip_ref, mixed_ref, gated_hbm, gated_ref, left):
    copies = []
    for index, (number, conv_ref) in enumerate(zip(numbers, convs)):
        halves = conv_ref.shape[0] // BLOCK
        for half in range(halves):
            columns = pl.ds(pl.multiple_of((number * halves + half) * LANES, LANES), LANES)
            mixed = mixed_ref[:, columns].astype(jnp.float32)
            conv = conv_ref[half * BLOCK : (half + 1) * BLOCK, :].T.astype(jnp.float32)
            summed = conv + skip_ref[:, columns] * mixed
            gated_ref[:, columns] = (query_ref[:, columns].astype(jnp.float32) * summed).astype(jnp.bfloat16)
        columns = pl.ds(pl.multiple_of(number * halves * LANES, halves * LANES), halves * LANES)
        copy = pltpu.make_async_copy(gated_ref.at[:, columns], gated_hbm.at[:, columns], left.at[index])
        copy.start()
        copies.append(copy)
    for copy in copies:
        copy.wait()


def gate_kernel(rounds, query_ref, skip_ref, mixed_ref, home_ref, *refs):
    conv_refs, (gated_hbm, gated_ref, left) = refs[: rounds.stop - rounds.start], refs[-3:]
    common = (query_ref, skip_ref, mixed_ref, gated_hbm, gated_ref, left)
    at_home = lax.axis_index("ctx") == 0

    @pl.when(jnp.logical_not(at_home))
    def _():
        gate_parts(partners(RETURN)[rounds], conv_refs, *common)

    if rounds.start == 0:

        @pl.when(at_home)
        def _():
            width = home_ref.shape[0] // LAGS
            gate_parts(range(LAGS), [home_ref.at[part * width : (part + 1) * width] for part in range(LAGS)], *common)


def per_device(query, key, value, filter_taps, skip):
    rows, channels = query.shape
    halves = channels // LAGS // LANES
    count = lax.axis_size("ctx")
    if count > LAGS:
        all_taps = lax.all_gather(filter_taps, "ctx", axis=0, tiled=True)
        first_tap = lax.axis_index("ctx") % LAGS * BLOCK
        filter_taps = lax.dynamic_slice_in_dim(all_taps, first_tap, BLOCK, axis=0)
    in_hbm = [pltpu.with_memory_space_constraint(array, pltpu.HBM) for array in (key, value, filter_taps)]
    whole = pl.BlockSpec(memory_space=pltpu.VMEM)
    *sent, mixed, home = pl.pallas_call(
        mix_kernel,
        out_shape=[jax.ShapeDtypeStruct((halves * BLOCK + TILE, LANES), jnp.bfloat16)] * LAGS
        + [jax.ShapeDtypeStruct(key.shape, jnp.bfloat16), jax.ShapeDtypeStruct((channels, rows), jnp.bfloat16)],
        in_specs=[pl.BlockSpec(memory_space=pl.ANY)] * 3,
        out_specs=[whole] * (LAGS + 2),
        scratch_shapes=[
            pltpu.VMEM(key.shape, key.dtype),
            pltpu.VMEM(value.shape, value.dtype),
            pltpu.VMEM(filter_taps.shape, filter_taps.dtype),
            pltpu.VMEM((LANES, BLOCK), jnp.bfloat16),
            pltpu.VMEM((LANES, BLOCK), jnp.float32),
            pltpu.SemaphoreType.DMA((5,)),
        ],
        compiler_params=SMALL,
    )(*in_hbm)
    got = exchange(sent, GATHER)
    sources = 1
    if count > LAGS:
        sources = 2
        onward = [(source, source + LAGS) for source in range(count - LAGS)]
        got = got + [lax.ppermute(block, "ctx", onward) for block in got]
    prepared = [
        jax.ShapeDtypeStruct((LAGS, TILE, BLOCK, LANES), jnp.bfloat16),
        jax.ShapeDtypeStruct((LAGS, halves * BLOCK, LANES), jnp.bfloat16),
    ]
    early = pl.pallas_call(
        early_kernel,
        out_shape=prepared,
        in_specs=[whole] * EARLY,
        out_specs=[whole] * 2,
        scratch_shapes=[pltpu.VMEM((EARLY, TILE, LANES), jnp.float32)],
        cost_estimate=pl.CostEstimate(flops=0, bytes_accessed=8 * 1024 * 1024, transcendentals=0),
        compiler_params=SMALL,
    )(*got[:EARLY])
    late = got[EARLY:]
    *conv, _, _ = pl.pallas_call(
        lambda *refs: conv_kernel(sources, *refs),
        out_shape=[jax.ShapeDtypeStruct((halves * BLOCK, LANES), jnp.bfloat16)] * LAGS + prepared,
        in_specs=[whole] * (len(late) + 2),
        out_specs=[whole] * (LAGS + 2),
        scratch_shapes=[
            pltpu.VMEM((TILE, LANES), jnp.float32),
            pltpu.VMEM((TILE, BLOCK, LANES), jnp.bfloat16),
            pltpu.VMEM((LAGS, halves * BLOCK, LANES), jnp.bfloat16),
        ],
        input_output_aliases={len(late): LAGS, len(late) + 1: LAGS + 1},
        compiler_params=SMALL,
    )(*late, *early)
    back = exchange(conv, RETURN)
    gated = None
    for rounds in (slice(0, FIRST), slice(FIRST, LAGS)):
        inputs = [query, skip.reshape(1, channels), mixed, home, *back[rounds]]
        specs = [whole] * len(inputs)
        if gated is not None:
            inputs.append(gated)
            specs.append(pl.BlockSpec(memory_space=pl.ANY))
        gated = pl.pallas_call(
            functools.partial(gate_kernel, rounds),
            out_shape=jax.ShapeDtypeStruct((rows, channels), jnp.bfloat16),
            in_specs=specs,
            out_specs=pl.BlockSpec(memory_space=pl.ANY),
            scratch_shapes=[pltpu.VMEM((rows, channels), jnp.bfloat16), pltpu.SemaphoreType.DMA((LAGS,))],
            input_output_aliases={} if gated is None else {len(inputs) - 1: 0},
            compiler_params=SMALL,
        )(*inputs)
    return gated


def solution(mesh):
    placed = (P("ctx", "ch"), P("ctx", "ch"), P("ctx", "ch"), P("ctx", "ch"), P("ch"))
    return jax.shard_map(
        per_device, mesh=mesh, in_specs=placed, out_specs=P("ctx", "ch"), check_vma=False
    )
```

```python
import functools

import jax
import jax.numpy as jnp
from jax import lax
from jax.experimental import pallas as pl
from jax.experimental.pallas import tpu as pltpu
from jax.sharding import PartitionSpec as P

GROUP = 16
BLOCK = 128
LAGS = 8
LANES = 128
TILE = 16
SIDE = LANES // GROUP
GATHER = ((6, 1, 4, 2, 5, 3, 7), (6, 1, 4, 2, 5, 3, 7))
RETURN = ((4, 1, 5, 2, 6, 3, 7), (4, 1, 5, 2, 6, 3, 7))
CHUNKS = 2
EARLY = 7
AHEAD = 4
UNROLL = 8
FIRST = 7
SMALL = pltpu.CompilerParams(vmem_limit_bytes=16 * 1024 * 1024)


def place():
    return lax.axis_index("ctx") % LAGS


def partners(orders):
    core = lax.axis_index("ch") % 2
    return [place()] + [place() ^ jnp.where(core == 0, first, second) for first, second in zip(*orders)]


def exchange(blocks, orders):
    size = lax.axis_size("ch")
    devices = range(lax.axis_size("ctx") * size)
    got = [blocks[0]]
    for block, steps in zip(blocks[1:], zip(*orders)):
        pairs = [(one, (one // size ^ steps[one % size % 2]) * size + one % size) for one in devices]
        got.append(lax.ppermute(block, ("ctx", "ch"), pairs))
    return got


def later_lanes():
    lane = lax.broadcasted_iota(jnp.int32, (BLOCK, LANES), 1)
    row = lax.broadcasted_iota(jnp.int32, (BLOCK, LANES), 0)
    return lane.astype(jnp.int16) >= row.astype(jnp.int16)


def mix_kernel(key_hbm, value_hbm, taps_hbm, *refs):
    sent_refs, refs = refs[:LAGS], refs[LAGS:]
    mixed_ref, home_ref, key_ref, value_ref, taps_ref, turned_ref, home_taps, arrived = refs
    halves = sent_refs[0].shape[0] // BLOCK
    width = halves * LANES
    taps_copy = pltpu.make_async_copy(taps_hbm, taps_ref, arrived.at[4])
    taps_copy.start()
    copies = []
    for index, first in enumerate((place() & 4 ^ 4, place() & 4)):
        columns = pl.ds(pl.multiple_of(first * width, width), 4 * width)
        pair = [
            pltpu.make_async_copy(key_hbm.at[:, columns], key_ref.at[:, columns], arrived.at[2 * index]),
            pltpu.make_async_copy(value_hbm.at[:, columns], value_ref.at[:, columns], arrived.at[2 * index + 1]),
        ]
        for copy in pair:
            copy.start()
        copies.append(pair)
    taps_copy.wait()
    turned_ref[...] = taps_ref[...].T
    parts = list(zip(partners(GATHER), sent_refs))
    for partner, sent_ref in parts:
        first = pl.multiple_of(partner * TILE, TILE)
        sent_ref[width : width + TILE, :] = turned_ref[pl.ds(first, TILE), :]
    steps = (0,) + GATHER[0]
    for pair, here in zip(copies, (True, False)):
        for copy in pair:
            copy.wait()
        for step, (partner, sent_ref) in zip(steps, parts):
            if (step >= 4) != here:
                continue
            for half in range(halves):
                columns = pl.ds(pl.multiple_of((partner * halves + half) * LANES, LANES), LANES)
                mixed = (
                    key_ref[:, columns].astype(jnp.float32) * value_ref[:, columns].astype(jnp.float32)
                ).astype(jnp.bfloat16)
                mixed_ref[:, columns] = mixed
                sent_ref[half * BLOCK : (half + 1) * BLOCK, :] = mixed.T

    @pl.when(lax.axis_index("ctx") == 0)
    def _():
        home_taps[...] = turned_ref[...].astype(jnp.float32)
        causal = later_lanes()
        for partner, sent_ref in parts:

            @pl.loop(0, TILE // 2, unroll=UNROLL)
            def _(pair):
                first = partner * TILE + 2 * pair
                rows = [circulant(home_taps[pl.ds(first + index, 1), :]) for index in range(2)]
                filters = [jnp.where(causal, row, jnp.zeros_like(row)) for row in rows]
                both = sent_ref[pl.ds(pl.multiple_of(2 * pair * GROUP, 2 * GROUP), 2 * GROUP), :]
                nothing = jnp.zeros((GROUP, LANES), jnp.bfloat16)
                signal = jnp.concatenate(
                    [
                        jnp.concatenate([both[0:GROUP], nothing], axis=0),
                        jnp.concatenate([nothing, both[GROUP : 2 * GROUP]], axis=0),
                    ],
                    axis=1,
                )
                total = jnp.dot(signal, jnp.concatenate(filters, axis=0), preferred_element_type=jnp.float32)
                there = pl.ds(pl.multiple_of(first * GROUP, 2 * GROUP), 2 * GROUP)
                home_ref[there, :] = total.astype(jnp.bfloat16)


def circulant(row):
    return pltpu.roll(jnp.broadcast_to(row, (BLOCK, LANES)), 0, 1, stride=1, stride_axis=0).astype(jnp.bfloat16)


def early_kernel(*refs):
    *got_refs, circulants, blocks, taps = refs
    width = blocks.shape[1]
    for index, (partner, got_ref) in enumerate(zip(partners(GATHER), got_refs)):
        taps[index] = got_ref[width : width + TILE, :].astype(jnp.float32)
        blocks[partner] = got_ref[0:width, :]

    @pl.loop(0, TILE, unroll=8)
    def _(group):
        for index, partner in enumerate(partners(GATHER)[:EARLY]):
            circulants[partner, group] = circulant(taps[index, pl.ds(group, 1), :])


def conv_kernel(sources, *refs):
    late_ref, *earlier_refs = refs[: 1 + (sources - 1) * LAGS]
    *conv_refs, circulants, blocks, taps, results, earlier = refs[1 + (sources - 1) * LAGS + 2 :]
    width = blocks.shape[1]
    late = partners(GATHER)[EARLY]
    taps[...] = late_ref[width : width + TILE, :].astype(jnp.float32)
    blocks[late] = late_ref[0:width, :]
    for partner, earlier_ref in zip(partners(GATHER), earlier_refs):
        earlier[partner] = earlier_ref[0:width, :]

    def add_late(group):
        circulants[late, group] = circulant(taps[group : group + 1, :])

    for group in range(AHEAD):
        add_late(group)
    causal = later_lanes()
    for group in range(TILE):
        if group + AHEAD < TILE:
            add_late(group + AHEAD)
        rows = slice(group * GROUP, (group + 1) * GROUP)
        before = jnp.zeros((BLOCK, LANES), jnp.bfloat16)
        filters, signals = [], []
        for lag in range(LAGS):
            turned = circulants[lag, group]
            filters.append(jnp.where(causal, turned, before))
            before = turned
            signal = [blocks[block, rows, :] for block in range(LAGS - lag)]
            if sources > 1:
                signal = [earlier[block, rows, :] for block in range(LAGS - lag, LAGS)] + signal
            elif lag:
                signal = [jnp.zeros((lag * GROUP, LANES), jnp.bfloat16)] + signal
            signals.append(jnp.concatenate(signal, axis=0))
        total = None
        for lag in range(0, LAGS, 2):
            skipped = lag * GROUP if sources == 1 else 0
            signal = jnp.concatenate([one[skipped:] for one in signals[lag : lag + 2]], axis=1)
            part = jnp.dot(signal, jnp.concatenate(filters[lag : lag + 2], axis=0), preferred_element_type=jnp.float32)
            if skipped:
                part = jnp.concatenate([total[:skipped], total[skipped:] + part], axis=0)
            elif lag:
                part = total + part
            total = part
        results[group] = total.astype(jnp.bfloat16)
    for partner, conv_ref in zip(partners(RETURN), conv_refs):
        rows = pl.ds(pl.multiple_of(partner * GROUP, GROUP), GROUP)
        for group in range(TILE):
            conv_ref[group * GROUP : (group + 1) * GROUP, :] = results[group, rows, :]


def gate_parts(numbers, convs, query_ref, skip_ref, mixed_ref, gated_hbm, gated_ref, left):
    copies = []
    for index, (number, conv_ref) in enumerate(zip(numbers, convs)):
        halves = conv_ref.shape[0] // BLOCK
        for half in range(halves):
            columns = pl.ds(pl.multiple_of((number * halves + half) * LANES, LANES), LANES)
            mixed = mixed_ref[:, columns].astype(jnp.float32)
            conv = conv_ref[half * BLOCK : (half + 1) * BLOCK, :].T.astype(jnp.float32)
            summed = conv + skip_ref[:, columns] * mixed
            gated_ref[:, columns] = (query_ref[:, columns].astype(jnp.float32) * summed).astype(jnp.bfloat16)
        columns = pl.ds(pl.multiple_of(number * halves * LANES, halves * LANES), halves * LANES)
        copy = pltpu.make_async_copy(gated_ref.at[:, columns], gated_hbm.at[:, columns], left.at[index])
        copy.start()
        copies.append(copy)
    for copy in copies:
        copy.wait()


def gate_kernel(rounds, query_ref, skip_ref, mixed_ref, home_ref, *refs):
    conv_refs, (gated_hbm, gated_ref, left) = refs[: rounds.stop - rounds.start], refs[-3:]
    common = (query_ref, skip_ref, mixed_ref, gated_hbm, gated_ref, left)
    at_home = lax.axis_index("ctx") == 0

    @pl.when(jnp.logical_not(at_home))
    def _():
        gate_parts(partners(RETURN)[rounds], conv_refs, *common)

    if rounds.start == 0:

        @pl.when(at_home)
        def _():
            width = home_ref.shape[0] // LAGS
            gate_parts(range(LAGS), [home_ref.at[part * width : (part + 1) * width] for part in range(LAGS)], *common)


def per_device(query, key, value, filter_taps, skip):
    rows, channels = query.shape
    halves = channels // LAGS // LANES
    count = lax.axis_size("ctx")
    if count > LAGS:
        all_taps = lax.all_gather(filter_taps, "ctx", axis=0, tiled=True)
        first_tap = lax.axis_index("ctx") % LAGS * BLOCK
        filter_taps = lax.dynamic_slice_in_dim(all_taps, first_tap, BLOCK, axis=0)
    in_hbm = [pltpu.with_memory_space_constraint(array, pltpu.HBM) for array in (key, value, filter_taps)]
    whole = pl.BlockSpec(memory_space=pltpu.VMEM)
    *sent, mixed, home = pl.pallas_call(
        mix_kernel,
        out_shape=[jax.ShapeDtypeStruct((halves * BLOCK + TILE, LANES), jnp.bfloat16)] * LAGS
        + [jax.ShapeDtypeStruct(key.shape, jnp.bfloat16), jax.ShapeDtypeStruct((channels, rows), jnp.bfloat16)],
        in_specs=[pl.BlockSpec(memory_space=pl.ANY)] * 3,
        out_specs=[whole] * (LAGS + 2),
        scratch_shapes=[
            pltpu.VMEM(key.shape, key.dtype),
            pltpu.VMEM(value.shape, value.dtype),
            pltpu.VMEM(filter_taps.shape, filter_taps.dtype),
            pltpu.VMEM((LANES, BLOCK), jnp.bfloat16),
            pltpu.VMEM((LANES, BLOCK), jnp.float32),
            pltpu.SemaphoreType.DMA((5,)),
        ],
        compiler_params=SMALL,
    )(*in_hbm)
    got = exchange(sent, GATHER)
    sources = 1
    if count > LAGS:
        sources = 2
        onward = [(source, source + LAGS) for source in range(count - LAGS)]
        got = got + [lax.ppermute(block, "ctx", onward) for block in got]
    prepared = [
        jax.ShapeDtypeStruct((LAGS, TILE, BLOCK, LANES), jnp.bfloat16),
        jax.ShapeDtypeStruct((LAGS, halves * BLOCK, LANES), jnp.bfloat16),
    ]
    early = pl.pallas_call(
        early_kernel,
        out_shape=prepared,
        in_specs=[whole] * EARLY,
        out_specs=[whole] * 2,
        scratch_shapes=[pltpu.VMEM((EARLY, TILE, LANES), jnp.float32)],
        cost_estimate=pl.CostEstimate(flops=0, bytes_accessed=8 * 1024 * 1024, transcendentals=0),
        compiler_params=SMALL,
    )(*got[:EARLY])
    late = got[EARLY:]
    *conv, _, _ = pl.pallas_call(
        lambda *refs: conv_kernel(sources, *refs),
        out_shape=[jax.ShapeDtypeStruct((halves * BLOCK, LANES), jnp.bfloat16)] * LAGS + prepared,
        in_specs=[whole] * (len(late) + 2),
        out_specs=[whole] * (LAGS + 2),
        scratch_shapes=[
            pltpu.VMEM((TILE, LANES), jnp.float32),
            pltpu.VMEM((TILE, BLOCK, LANES), jnp.bfloat16),
            pltpu.VMEM((LAGS, halves * BLOCK, LANES), jnp.bfloat16),
        ],
        input_output_aliases={len(late): LAGS, len(late) + 1: LAGS + 1},
        compiler_params=SMALL,
    )(*late, *early)
    back = exchange(conv, RETURN)
    gated = None
    for rounds in (slice(0, FIRST), slice(FIRST, LAGS)):
        inputs = [query, skip.reshape(1, channels), mixed, home, *back[rounds]]
        specs = [whole] * len(inputs)
        if gated is not None:
            inputs.append(gated)
            specs.append(pl.BlockSpec(memory_space=pl.ANY))
        gated = pl.pallas_call(
            functools.partial(gate_kernel, rounds),
            out_shape=jax.ShapeDtypeStruct((rows, channels), jnp.bfloat16),
            in_specs=specs,
            out_specs=pl.BlockSpec(memory_space=pl.ANY),
            scratch_shapes=[pltpu.VMEM((rows, channels), jnp.bfloat16), pltpu.SemaphoreType.DMA((LAGS,))],
            input_output_aliases={} if gated is None else {len(inputs) - 1: 0},
            compiler_params=SMALL,
        )(*inputs)
    return gated


def solution(mesh):
    placed = (P("ctx", "ch"), P("ctx", "ch"), P("ctx", "ch"), P("ctx", "ch"), P("ch"))
    return jax.shard_map(
        per_device, mesh=mesh, in_specs=placed, out_specs=P("ctx", "ch"), check_vma=False
    )
```

```python
import functools

import jax
import jax.numpy as jnp
from jax import lax
from jax.experimental import pallas as pl
from jax.experimental.pallas import tpu as pltpu
from jax.sharding import PartitionSpec as P

GROUP = 16
BLOCK = 128
LAGS = 8
LANES = 128
TILE = 16
SIDE = LANES // GROUP
GATHER = ((6, 1, 4, 2, 5, 3, 7), (6, 1, 4, 2, 5, 3, 7))
RETURN = ((4, 1, 7, 2, 6, 3, 5), (4, 1, 7, 2, 6, 3, 5))
CHUNKS = 2
EARLY = 7
AHEAD = 4
UNROLL = 8
FIRST = 7
SMALL = pltpu.CompilerParams(vmem_limit_bytes=16 * 1024 * 1024)


def place():
    return lax.axis_index("ctx") % LAGS


def partners(orders):
    core = lax.axis_index("ch") % 2
    return [place()] + [place() ^ jnp.where(core == 0, first, second) for first, second in zip(*orders)]


def exchange(blocks, orders):
    size = lax.axis_size("ch")
    devices = range(lax.axis_size("ctx") * size)
    got = [blocks[0]]
    for block, steps in zip(blocks[1:], zip(*orders)):
        pairs = [(one, (one // size ^ steps[one % size % 2]) * size + one % size) for one in devices]
        got.append(lax.ppermute(block, ("ctx", "ch"), pairs))
    return got


def later_lanes():
    lane = lax.broadcasted_iota(jnp.int32, (BLOCK, LANES), 1)
    row = lax.broadcasted_iota(jnp.int32, (BLOCK, LANES), 0)
    return lane.astype(jnp.int16) >= row.astype(jnp.int16)


def mix_kernel(key_hbm, value_hbm, taps_hbm, *refs):
    sent_refs, refs = refs[:LAGS], refs[LAGS:]
    mixed_ref, home_ref, key_ref, value_ref, taps_ref, turned_ref, home_taps, arrived = refs
    halves = sent_refs[0].shape[0] // BLOCK
    width = halves * LANES
    taps_copy = pltpu.make_async_copy(taps_hbm, taps_ref, arrived.at[4])
    taps_copy.start()
    copies = []
    for index, first in enumerate((place() & 4 ^ 4, place() & 4)):
        columns = pl.ds(pl.multiple_of(first * width, width), 4 * width)
        pair = [
            pltpu.make_async_copy(key_hbm.at[:, columns], key_ref.at[:, columns], arrived.at[2 * index]),
            pltpu.make_async_copy(value_hbm.at[:, columns], value_ref.at[:, columns], arrived.at[2 * index + 1]),
        ]
        for copy in pair:
            copy.start()
        copies.append(pair)
    taps_copy.wait()
    turned_ref[...] = taps_ref[...].T
    parts = list(zip(partners(GATHER), sent_refs))
    for partner, sent_ref in parts:
        first = pl.multiple_of(partner * TILE, TILE)
        sent_ref[width : width + TILE, :] = turned_ref[pl.ds(first, TILE), :]
    steps = (0,) + GATHER[0]
    for pair, here in zip(copies, (True, False)):
        for copy in pair:
            copy.wait()
        for step, (partner, sent_ref) in zip(steps, parts):
            if (step >= 4) != here:
                continue
            for half in range(halves):
                columns = pl.ds(pl.multiple_of((partner * halves + half) * LANES, LANES), LANES)
                mixed = (
                    key_ref[:, columns].astype(jnp.float32) * value_ref[:, columns].astype(jnp.float32)
                ).astype(jnp.bfloat16)
                mixed_ref[:, columns] = mixed
                sent_ref[half * BLOCK : (half + 1) * BLOCK, :] = mixed.T

    @pl.when(lax.axis_index("ctx") == 0)
    def _():
        home_taps[...] = turned_ref[...].astype(jnp.float32)
        causal = later_lanes()
        for partner, sent_ref in parts:

            @pl.loop(0, TILE // 2, unroll=UNROLL)
            def _(pair):
                first = partner * TILE + 2 * pair
                rows = [circulant(home_taps[pl.ds(first + index, 1), :]) for index in range(2)]
                filters = [jnp.where(causal, row, jnp.zeros_like(row)) for row in rows]
                both = sent_ref[pl.ds(pl.multiple_of(2 * pair * GROUP, 2 * GROUP), 2 * GROUP), :]
                nothing = jnp.zeros((GROUP, LANES), jnp.bfloat16)
                signal = jnp.concatenate(
                    [
                        jnp.concatenate([both[0:GROUP], nothing], axis=0),
                        jnp.concatenate([nothing, both[GROUP : 2 * GROUP]], axis=0),
                    ],
                    axis=1,
                )
                total = jnp.dot(signal, jnp.concatenate(filters, axis=0), preferred_element_type=jnp.float32)
                there = pl.ds(pl.multiple_of(first * GROUP, 2 * GROUP), 2 * GROUP)
                home_ref[there, :] = total.astype(jnp.bfloat16)


def circulant(row):
    return pltpu.roll(jnp.broadcast_to(row, (BLOCK, LANES)), 0, 1, stride=1, stride_axis=0).astype(jnp.bfloat16)


def early_kernel(*refs):
    *got_refs, circulants, blocks, taps = refs
    width = blocks.shape[1]
    for index, (partner, got_ref) in enumerate(zip(partners(GATHER), got_refs)):
        taps[index] = got_ref[width : width + TILE, :].astype(jnp.float32)
        blocks[partner] = got_ref[0:width, :]

    @pl.loop(0, TILE, unroll=8)
    def _(group):
        for index, partner in enumerate(partners(GATHER)[:EARLY]):
            circulants[partner, group] = circulant(taps[index, pl.ds(group, 1), :])


def conv_kernel(sources, *refs):
    late_ref, *earlier_refs = refs[: 1 + (sources - 1) * LAGS]
    *conv_refs, circulants, blocks, taps, results, earlier = refs[1 + (sources - 1) * LAGS + 2 :]
    width = blocks.shape[1]
    late = partners(GATHER)[EARLY]
    taps[...] = late_ref[width : width + TILE, :].astype(jnp.float32)
    blocks[late] = late_ref[0:width, :]
    for partner, earlier_ref in zip(partners(GATHER), earlier_refs):
        earlier[partner] = earlier_ref[0:width, :]

    def add_late(group):
        circulants[late, group] = circulant(taps[group : group + 1, :])

    for group in range(AHEAD):
        add_late(group)
    causal = later_lanes()
    for group in range(TILE):
        if group + AHEAD < TILE:
            add_late(group + AHEAD)
        rows = slice(group * GROUP, (group + 1) * GROUP)
        before = jnp.zeros((BLOCK, LANES), jnp.bfloat16)
        filters, signals = [], []
        for lag in range(LAGS):
            turned = circulants[lag, group]
            filters.append(jnp.where(causal, turned, before))
            before = turned
            signal = [blocks[block, rows, :] for block in range(LAGS - lag)]
            if sources > 1:
                signal = [earlier[block, rows, :] for block in range(LAGS - lag, LAGS)] + signal
            elif lag:
                signal = [jnp.zeros((lag * GROUP, LANES), jnp.bfloat16)] + signal
            signals.append(jnp.concatenate(signal, axis=0))
        total = None
        for lag in range(0, LAGS, 2):
            skipped = lag * GROUP if sources == 1 else 0
            signal = jnp.concatenate([one[skipped:] for one in signals[lag : lag + 2]], axis=1)
            part = jnp.dot(signal, jnp.concatenate(filters[lag : lag + 2], axis=0), preferred_element_type=jnp.float32)
            if skipped:
                part = jnp.concatenate([total[:skipped], total[skipped:] + part], axis=0)
            elif lag:
                part = total + part
            total = part
        results[group] = total.astype(jnp.bfloat16)
    for partner, conv_ref in zip(partners(RETURN), conv_refs):
        rows = pl.ds(pl.multiple_of(partner * GROUP, GROUP), GROUP)
        for group in range(TILE):
            conv_ref[group * GROUP : (group + 1) * GROUP, :] = results[group, rows, :]


def gate_parts(numbers, convs, query_ref, skip_ref, mixed_ref, gated_hbm, gated_ref, left):
    copies = []
    for index, (number, conv_ref) in enumerate(zip(numbers, convs)):
        halves = conv_ref.shape[0] // BLOCK
        for half in range(halves):
            columns = pl.ds(pl.multiple_of((number * halves + half) * LANES, LANES), LANES)
            mixed = mixed_ref[:, columns].astype(jnp.float32)
            conv = conv_ref[half * BLOCK : (half + 1) * BLOCK, :].T.astype(jnp.float32)
            summed = conv + skip_ref[:, columns] * mixed
            gated_ref[:, columns] = (query_ref[:, columns].astype(jnp.float32) * summed).astype(jnp.bfloat16)
        columns = pl.ds(pl.multiple_of(number * halves * LANES, halves * LANES), halves * LANES)
        copy = pltpu.make_async_copy(gated_ref.at[:, columns], gated_hbm.at[:, columns], left.at[index])
        copy.start()
        copies.append(copy)
    for copy in copies:
        copy.wait()


def gate_kernel(rounds, query_ref, skip_ref, mixed_ref, home_ref, *refs):
    conv_refs, (gated_hbm, gated_ref, left) = refs[: rounds.stop - rounds.start], refs[-3:]
    common = (query_ref, skip_ref, mixed_ref, gated_hbm, gated_ref, left)
    at_home = lax.axis_index("ctx") == 0

    @pl.when(jnp.logical_not(at_home))
    def _():
        gate_parts(partners(RETURN)[rounds], conv_refs, *common)

    if rounds.start == 0:

        @pl.when(at_home)
        def _():
            width = home_ref.shape[0] // LAGS
            gate_parts(range(LAGS), [home_ref.at[part * width : (part + 1) * width] for part in range(LAGS)], *common)


def per_device(query, key, value, filter_taps, skip):
    rows, channels = query.shape
    halves = channels // LAGS // LANES
    count = lax.axis_size("ctx")
    if count > LAGS:
        all_taps = lax.all_gather(filter_taps, "ctx", axis=0, tiled=True)
        first_tap = lax.axis_index("ctx") % LAGS * BLOCK
        filter_taps = lax.dynamic_slice_in_dim(all_taps, first_tap, BLOCK, axis=0)
    in_hbm = [pltpu.with_memory_space_constraint(array, pltpu.HBM) for array in (key, value, filter_taps)]
    whole = pl.BlockSpec(memory_space=pltpu.VMEM)
    *sent, mixed, home = pl.pallas_call(
        mix_kernel,
        out_shape=[jax.ShapeDtypeStruct((halves * BLOCK + TILE, LANES), jnp.bfloat16)] * LAGS
        + [jax.ShapeDtypeStruct(key.shape, jnp.bfloat16), jax.ShapeDtypeStruct((channels, rows), jnp.bfloat16)],
        in_specs=[pl.BlockSpec(memory_space=pl.ANY)] * 3,
        out_specs=[whole] * (LAGS + 2),
        scratch_shapes=[
            pltpu.VMEM(key.shape, key.dtype),
            pltpu.VMEM(value.shape, value.dtype),
            pltpu.VMEM(filter_taps.shape, filter_taps.dtype),
            pltpu.VMEM((LANES, BLOCK), jnp.bfloat16),
            pltpu.VMEM((LANES, BLOCK), jnp.float32),
            pltpu.SemaphoreType.DMA((5,)),
        ],
        compiler_params=SMALL,
    )(*in_hbm)
    got = exchange(sent, GATHER)
    sources = 1
    if count > LAGS:
        sources = 2
        onward = [(source, source + LAGS) for source in range(count - LAGS)]
        got = got + [lax.ppermute(block, "ctx", onward) for block in got]
    prepared = [
        jax.ShapeDtypeStruct((LAGS, TILE, BLOCK, LANES), jnp.bfloat16),
        jax.ShapeDtypeStruct((LAGS, halves * BLOCK, LANES), jnp.bfloat16),
    ]
    early = pl.pallas_call(
        early_kernel,
        out_shape=prepared,
        in_specs=[whole] * EARLY,
        out_specs=[whole] * 2,
        scratch_shapes=[pltpu.VMEM((EARLY, TILE, LANES), jnp.float32)],
        cost_estimate=pl.CostEstimate(flops=0, bytes_accessed=8 * 1024 * 1024, transcendentals=0),
        compiler_params=SMALL,
    )(*got[:EARLY])
    late = got[EARLY:]
    *conv, _, _ = pl.pallas_call(
        lambda *refs: conv_kernel(sources, *refs),
        out_shape=[jax.ShapeDtypeStruct((halves * BLOCK, LANES), jnp.bfloat16)] * LAGS + prepared,
        in_specs=[whole] * (len(late) + 2),
        out_specs=[whole] * (LAGS + 2),
        scratch_shapes=[
            pltpu.VMEM((TILE, LANES), jnp.float32),
            pltpu.VMEM((TILE, BLOCK, LANES), jnp.bfloat16),
            pltpu.VMEM((LAGS, halves * BLOCK, LANES), jnp.bfloat16),
        ],
        input_output_aliases={len(late): LAGS, len(late) + 1: LAGS + 1},
        compiler_params=SMALL,
    )(*late, *early)
    back = exchange(conv, RETURN)
    gated = None
    for rounds in (slice(0, FIRST), slice(FIRST, LAGS)):
        inputs = [query, skip.reshape(1, channels), mixed, home, *back[rounds]]
        specs = [whole] * len(inputs)
        if gated is not None:
            inputs.append(gated)
            specs.append(pl.BlockSpec(memory_space=pl.ANY))
        gated = pl.pallas_call(
            functools.partial(gate_kernel, rounds),
            out_shape=jax.ShapeDtypeStruct((rows, channels), jnp.bfloat16),
            in_specs=specs,
            out_specs=pl.BlockSpec(memory_space=pl.ANY),
            scratch_shapes=[pltpu.VMEM((rows, channels), jnp.bfloat16), pltpu.SemaphoreType.DMA((LAGS,))],
            input_output_aliases={} if gated is None else {len(inputs) - 1: 0},
            compiler_params=SMALL,
        )(*inputs)
    return gated


def solution(mesh):
    placed = (P("ctx", "ch"), P("ctx", "ch"), P("ctx", "ch"), P("ctx", "ch"), P("ch"))
    return jax.shard_map(
        per_device, mesh=mesh, in_specs=placed, out_specs=P("ctx", "ch"), check_vma=False
    )
```

```python
import functools

import jax
import jax.numpy as jnp
from jax import lax
from jax.experimental import pallas as pl
from jax.experimental.pallas import tpu as pltpu
from jax.sharding import PartitionSpec as P

GROUP = 16
BLOCK = 128
LAGS = 8
LANES = 128
TILE = 16
SIDE = LANES // GROUP
GATHER = ((6, 1, 4, 2, 5, 3, 7), (6, 1, 4, 2, 5, 3, 7))
RETURN = ((4, 1, 7, 2, 6, 3, 5), (4, 1, 7, 2, 6, 3, 5))
CHUNKS = 2
EARLY = 7
UNROLL = 8
FIRST = 7
SMALL = pltpu.CompilerParams(vmem_limit_bytes=16 * 1024 * 1024)


def place():
    return lax.axis_index("ctx") % LAGS


def partners(orders):
    core = lax.axis_index("ch") % 2
    return [place()] + [place() ^ jnp.where(core == 0, first, second) for first, second in zip(*orders)]


def exchange(blocks, orders):
    size = lax.axis_size("ch")
    devices = range(lax.axis_size("ctx") * size)
    got = [blocks[0]]
    for block, steps in zip(blocks[1:], zip(*orders)):
        pairs = [(one, (one // size ^ steps[one % size % 2]) * size + one % size) for one in devices]
        got.append(lax.ppermute(block, ("ctx", "ch"), pairs))
    return got


def later_lanes():
    lane = lax.broadcasted_iota(jnp.int32, (BLOCK, LANES), 1)
    row = lax.broadcasted_iota(jnp.int32, (BLOCK, LANES), 0)
    return lane.astype(jnp.int16) >= row.astype(jnp.int16)


def mix_kernel(key_hbm, value_hbm, taps_hbm, *refs):
    sent_refs, refs = refs[:LAGS], refs[LAGS:]
    mixed_ref, home_ref, key_ref, value_ref, taps_ref, turned_ref, home_taps, arrived = refs
    halves = sent_refs[0].shape[0] // BLOCK
    width = halves * LANES
    taps_copy = pltpu.make_async_copy(taps_hbm, taps_ref, arrived.at[4])
    taps_copy.start()
    copies = []
    for index, first in enumerate((place() & 4 ^ 4, place() & 4)):
        columns = pl.ds(pl.multiple_of(first * width, width), 4 * width)
        pair = [
            pltpu.make_async_copy(key_hbm.at[:, columns], key_ref.at[:, columns], arrived.at[2 * index]),
            pltpu.make_async_copy(value_hbm.at[:, columns], value_ref.at[:, columns], arrived.at[2 * index + 1]),
        ]
        for copy in pair:
            copy.start()
        copies.append(pair)
    taps_copy.wait()
    turned_ref[...] = taps_ref[...].T
    parts = list(zip(partners(GATHER), sent_refs))
    for partner, sent_ref in parts:
        first = pl.multiple_of(partner * TILE, TILE)
        sent_ref[width : width + TILE, :] = turned_ref[pl.ds(first, TILE), :]
    steps = (0,) + GATHER[0]
    for pair, here in zip(copies, (True, False)):
        for copy in pair:
            copy.wait()
        for step, (partner, sent_ref) in zip(steps, parts):
            if (step >= 4) != here:
                continue
            for half in range(halves):
                columns = pl.ds(pl.multiple_of((partner * halves + half) * LANES, LANES), LANES)
                mixed = (
                    key_ref[:, columns].astype(jnp.float32) * value_ref[:, columns].astype(jnp.float32)
                ).astype(jnp.bfloat16)
                mixed_ref[:, columns] = mixed
                sent_ref[half * BLOCK : (half + 1) * BLOCK, :] = mixed.T

    @pl.when(lax.axis_index("ctx") == 0)
    def _():
        home_taps[...] = turned_ref[...].astype(jnp.float32)
        causal = later_lanes()
        for partner, sent_ref in parts:

            @pl.loop(0, TILE // 2, unroll=UNROLL)
            def _(pair):
                first = partner * TILE + 2 * pair
                rows = [circulant(home_taps[pl.ds(first + index, 1), :]) for index in range(2)]
                filters = [jnp.where(causal, row, jnp.zeros_like(row)) for row in rows]
                both = sent_ref[pl.ds(pl.multiple_of(2 * pair * GROUP, 2 * GROUP), 2 * GROUP), :]
                nothing = jnp.zeros((GROUP, LANES), jnp.bfloat16)
                signal = jnp.concatenate(
                    [
                        jnp.concatenate([both[0:GROUP], nothing], axis=0),
                        jnp.concatenate([nothing, both[GROUP : 2 * GROUP]], axis=0),
                    ],
                    axis=1,
                )
                total = jnp.dot(signal, jnp.concatenate(filters, axis=0), preferred_element_type=jnp.float32)
                there = pl.ds(pl.multiple_of(first * GROUP, 2 * GROUP), 2 * GROUP)
                home_ref[there, :] = total.astype(jnp.bfloat16)


def circulant(row):
    return pltpu.roll(jnp.broadcast_to(row, (BLOCK, LANES)), 0, 1, stride=1, stride_axis=0).astype(jnp.bfloat16)


def early_kernel(*refs):
    *got_refs, circulants, blocks, taps = refs
    width = blocks.shape[1]
    for index, (partner, got_ref) in enumerate(zip(partners(GATHER), got_refs)):
        taps[index] = got_ref[width : width + TILE, :].astype(jnp.float32)
        blocks[partner] = got_ref[0:width, :]

    @pl.loop(0, TILE, unroll=8)
    def _(group):
        for index, partner in enumerate(partners(GATHER)[:EARLY]):
            circulants[partner, group] = circulant(taps[index, pl.ds(group, 1), :])


def conv_kernel(sources, *refs):
    late_ref, *earlier_refs = refs[: 1 + (sources - 1) * LAGS]
    circulants, early_blocks, *conv_refs, taps, results, blocks, earlier = refs[1 + (sources - 1) * LAGS :]
    width = blocks.shape[1]
    late = partners(GATHER)[EARLY]
    taps[...] = late_ref[width : width + TILE, :].astype(jnp.float32)
    blocks[...] = early_blocks[...]
    blocks[late] = late_ref[0:width, :]
    for partner, earlier_ref in zip(partners(GATHER), earlier_refs):
        earlier[partner] = earlier_ref[0:width, :]

    causal = later_lanes()
    for group in range(TILE):
        newest = circulant(taps[group : group + 1, :])
        rows = slice(group * GROUP, (group + 1) * GROUP)
        before = jnp.zeros((BLOCK, LANES), jnp.bfloat16)
        filters, signals = [], []
        for lag in range(LAGS):
            turned = jnp.where(lag == late, newest, circulants[lag, group])
            filters.append(jnp.where(causal, turned, before))
            before = turned
            signal = [blocks[block, rows, :] for block in range(LAGS - lag)]
            if sources > 1:
                signal = [earlier[block, rows, :] for block in range(LAGS - lag, LAGS)] + signal
            elif lag:
                signal = [jnp.zeros((lag * GROUP, LANES), jnp.bfloat16)] + signal
            signals.append(jnp.concatenate(signal, axis=0))
        total = None
        for lag in range(0, LAGS, 2):
            skipped = lag * GROUP if sources == 1 else 0
            signal = jnp.concatenate([one[skipped:] for one in signals[lag : lag + 2]], axis=1)
            part = jnp.dot(signal, jnp.concatenate(filters[lag : lag + 2], axis=0), preferred_element_type=jnp.float32)
            if skipped:
                part = jnp.concatenate([total[:skipped], total[skipped:] + part], axis=0)
            elif lag:
                part = total + part
            total = part
        results[group] = total.astype(jnp.bfloat16)
    for partner, conv_ref in zip(partners(RETURN), conv_refs):
        rows = pl.ds(pl.multiple_of(partner * GROUP, GROUP), GROUP)
        for group in range(TILE):
            conv_ref[group * GROUP : (group + 1) * GROUP, :] = results[group, rows, :]


def gate_parts(numbers, convs, query_ref, skip_ref, mixed_ref, gated_hbm, gated_ref, left):
    copies = []
    for index, (number, conv_ref) in enumerate(zip(numbers, convs)):
        halves = conv_ref.shape[0] // BLOCK
        for half in range(halves):
            columns = pl.ds(pl.multiple_of((number * halves + half) * LANES, LANES), LANES)
            mixed = mixed_ref[:, columns].astype(jnp.float32)
            conv = conv_ref[half * BLOCK : (half + 1) * BLOCK, :].T.astype(jnp.float32)
            summed = conv + skip_ref[:, columns] * mixed
            gated_ref[:, columns] = (query_ref[:, columns].astype(jnp.float32) * summed).astype(jnp.bfloat16)
        columns = pl.ds(pl.multiple_of(number * halves * LANES, halves * LANES), halves * LANES)
        copy = pltpu.make_async_copy(gated_ref.at[:, columns], gated_hbm.at[:, columns], left.at[index])
        copy.start()
        copies.append(copy)
    for copy in copies:
        copy.wait()


def gate_kernel(rounds, query_ref, skip_ref, mixed_ref, home_ref, *refs):
    conv_refs, (gated_hbm, gated_ref, left) = refs[: rounds.stop - rounds.start], refs[-3:]
    common = (query_ref, skip_ref, mixed_ref, gated_hbm, gated_ref, left)
    at_home = lax.axis_index("ctx") == 0

    @pl.when(jnp.logical_not(at_home))
    def _():
        gate_parts(partners(RETURN)[rounds], conv_refs, *common)

    if rounds.start == 0:

        @pl.when(at_home)
        def _():
            width = home_ref.shape[0] // LAGS
            gate_parts(range(LAGS), [home_ref.at[part * width : (part + 1) * width] for part in range(LAGS)], *common)


def per_device(query, key, value, filter_taps, skip):
    rows, channels = query.shape
    halves = channels // LAGS // LANES
    count = lax.axis_size("ctx")
    if count > LAGS:
        all_taps = lax.all_gather(filter_taps, "ctx", axis=0, tiled=True)
        first_tap = lax.axis_index("ctx") % LAGS * BLOCK
        filter_taps = lax.dynamic_slice_in_dim(all_taps, first_tap, BLOCK, axis=0)
    in_hbm = [pltpu.with_memory_space_constraint(array, pltpu.HBM) for array in (key, value, filter_taps)]
    whole = pl.BlockSpec(memory_space=pltpu.VMEM)
    *sent, mixed, home = pl.pallas_call(
        mix_kernel,
        out_shape=[jax.ShapeDtypeStruct((halves * BLOCK + TILE, LANES), jnp.bfloat16)] * LAGS
        + [jax.ShapeDtypeStruct(key.shape, jnp.bfloat16), jax.ShapeDtypeStruct((channels, rows), jnp.bfloat16)],
        in_specs=[pl.BlockSpec(memory_space=pl.ANY)] * 3,
        out_specs=[whole] * (LAGS + 2),
        scratch_shapes=[
            pltpu.VMEM(key.shape, key.dtype),
            pltpu.VMEM(value.shape, value.dtype),
            pltpu.VMEM(filter_taps.shape, filter_taps.dtype),
            pltpu.VMEM((LANES, BLOCK), jnp.bfloat16),
            pltpu.VMEM((LANES, BLOCK), jnp.float32),
            pltpu.SemaphoreType.DMA((5,)),
        ],
        compiler_params=SMALL,
    )(*in_hbm)
    got = exchange(sent, GATHER)
    sources = 1
    if count > LAGS:
        sources = 2
        onward = [(source, source + LAGS) for source in range(count - LAGS)]
        got = got + [lax.ppermute(block, "ctx", onward) for block in got]
    prepared = [
        jax.ShapeDtypeStruct((LAGS, TILE, BLOCK, LANES), jnp.bfloat16),
        jax.ShapeDtypeStruct((LAGS, halves * BLOCK, LANES), jnp.bfloat16),
    ]
    early = pl.pallas_call(
        early_kernel,
        out_shape=prepared,
        in_specs=[whole] * EARLY,
        out_specs=[whole] * 2,
        scratch_shapes=[pltpu.VMEM((EARLY, TILE, LANES), jnp.float32)],
        cost_estimate=pl.CostEstimate(flops=0, bytes_accessed=8 * 1024 * 1024, transcendentals=0),
        compiler_params=SMALL,
    )(*got[:EARLY])
    late = got[EARLY:]
    conv = pl.pallas_call(
        lambda *refs: conv_kernel(sources, *refs),
        out_shape=[jax.ShapeDtypeStruct((halves * BLOCK, LANES), jnp.bfloat16)] * LAGS,
        in_specs=[whole] * (len(late) + 2),
        out_specs=[whole] * LAGS,
        scratch_shapes=[
            pltpu.VMEM((TILE, LANES), jnp.float32),
            pltpu.VMEM((TILE, BLOCK, LANES), jnp.bfloat16),
            pltpu.VMEM((LAGS, halves * BLOCK, LANES), jnp.bfloat16),
            pltpu.VMEM((LAGS, halves * BLOCK, LANES), jnp.bfloat16),
        ],
        compiler_params=SMALL,
    )(*late, *early)
    back = exchange(conv, RETURN)
    gated = None
    for rounds in (slice(0, FIRST), slice(FIRST, LAGS)):
        inputs = [query, skip.reshape(1, channels), mixed, home, *back[rounds]]
        specs = [whole] * len(inputs)
        if gated is not None:
            inputs.append(gated)
            specs.append(pl.BlockSpec(memory_space=pl.ANY))
        gated = pl.pallas_call(
            functools.partial(gate_kernel, rounds),
            out_shape=jax.ShapeDtypeStruct((rows, channels), jnp.bfloat16),
            in_specs=specs,
            out_specs=pl.BlockSpec(memory_space=pl.ANY),
            scratch_shapes=[pltpu.VMEM((rows, channels), jnp.bfloat16), pltpu.SemaphoreType.DMA((LAGS,))],
            input_output_aliases={} if gated is None else {len(inputs) - 1: 0},
            compiler_params=SMALL,
        )(*inputs)
    return gated


def solution(mesh):
    placed = (P("ctx", "ch"), P("ctx", "ch"), P("ctx", "ch"), P("ctx", "ch"), P("ch"))
    return jax.shard_map(
        per_device, mesh=mesh, in_specs=placed, out_specs=P("ctx", "ch"), check_vma=False
    )
```
